768 devices in a mesh: dp: 12 (over z), expert: 64 (over x, y, core).
Axes of the slice: x: 4, y: 8, z: 12, core: 2. Of those that a mesh axis runs over, the one named last changes fastest.
Arguments:
- tokens: bfloat16 [1024, 4096], P('expert'), may hold values from -6 to 6
- route: int32 [1024, 8], P('expert'), may hold values from 0 to 63, all different within a row; in each aligned block of 16 rows (0 to 15, 16 to 31, ...) at most 2 rows name the same one
- gate_code: int32 [1024, 8], P('expert'), may hold values from 1 to 999
- cotangent: bfloat16 [1024, 4096], P('expert'), may hold values from -6 to 6
- w_gate: bfloat16 [64, 4096, 1536], P('expert', None, 'dp'), may hold values from -0.09375 to 0.09375
- w_up: bfloat16 [64, 4096, 1536], P('expert', None, 'dp'), may hold values from -0.09375 to 0.09375
- w_down: bfloat16 [64, 1536, 4096], P('expert', 'dp'), may hold values from -0.15625 to 0.15625
Outputs:
- mixed: bfloat16 [1024, 4096], P('expert')
- grad_tokens: bfloat16 [1024, 4096], P('expert')
- grad_gates: float32 [1024, 8], P('expert')
- grad_down: bfloat16 [64, 1536, 4096], P('expert', 'dp')
The draws below stay inside these ranges and needn't reach their ends.
Inputs may be any that keep to these rules, and one draw needn't show every extreme that they name: `route`: each row names 8 different experts. Within the 16 rows of one device no expert is named more than 2 times, and in some device's rows some expert is named exactly 2 times.
All inputs are finite; a program needn't handle non-finite values.
Results may differ from the reference program's by a relative error of at most 0.023.
Values may be sent and summed in bfloat16 or wider, within the bound.
A program may use at most 64 MiB of HBM per device.

```python
import math
import jax
import jax.numpy as jnp
import numpy as np
from jax import lax

D = 4096
FF = 1536
TOP = 8
TOK_DEV = 16
EXPERTS = 64
TOKENS = 1024
CAP = 2
FD = 128
N_DP = 12
N_EXPERT = 64


def set_ends(entries, key, smallest, high):
    shape = entries.shape
    index_at = [jax.random.randint(jax.random.fold_in(key, axis), (), 0, shape[axis]) for axis in range(len(shape))]
    entries = entries.at[tuple(index_at)].set(smallest)
    longest = shape.index(max(shape))
    index_at[longest] = (index_at[longest] + 1) % shape[longest]
    return entries.at[tuple(index_at)].set(high)


def steps_of(key, shape, cuts, smallest, largest):
    def one(axis_at, shards_of):
        steps = jax.random.uniform(jax.random.fold_in(jax.random.fold_in(key, 6), axis_at), (shards_of,), jnp.float32, smallest / len(cuts), largest / len(cuts))
        return jnp.repeat(jnp.exp(steps), shape[axis_at] // shards_of).reshape((-1,) + (1,) * (len(shape) - axis_at - 1))

    loudness = one(*cuts[0])
    for cut in cuts[1:]:
        loudness = loudness * one(*cut)
    return loudness


def assign_block(key, own, number, rows, number_of, top, limit, skew):
    order = jax.random.permutation(key, number_of)
    heavy_load, common = portions_of(number_of, rows * top, limit, skew, True), portions_of(number_of, rows * top, limit, skew, False)
    places = jnp.arange(number_of)

    def named(sizes, rotation):
        used = int((sizes > 0).sum())
        fixed = max(1, used // 4)
        passed = fixed + (places - fixed + rotation * (used - fixed)) % max(1, number_of - fixed)
        return jnp.zeros((number_of,), jnp.int32).at[order[jnp.where(places < fixed, places, passed)]].set(jnp.asarray(sizes, jnp.int32))

    sizes = jnp.where(number % 4 == 0, named(heavy_load, number // 4), named(common, number - number // 4 - 1))
    mixed = jax.random.permutation(jax.random.fold_in(own, 3), number_of)
    giver, sink = mixed[0:number_of // 2 * 2:2], mixed[1:number_of // 2 * 2:2]
    margin = jnp.minimum(sizes[giver] - 1, limit - sizes[sink]) // 2
    margin = jnp.where((giver == order[0]) | (sink == order[0]) | (sizes[sink] == 0), 0, jnp.maximum(margin, 0))
    passed = jax.random.randint(jax.random.fold_in(own, 4), (number_of // 2,), 0, 1 << 20) % (margin + 1)
    sizes = sizes.at[giver].add(-passed).at[sink].add(passed)
    items = jnp.searchsorted(jnp.cumsum(sizes), jnp.arange(rows * top), side="right").astype(jnp.int32)
    table = items.reshape(top, rows).T
    table = table[jax.random.permutation(jax.random.fold_in(own, 1), rows)]
    rotation = jax.random.randint(jax.random.fold_in(own, 2), (rows, 1), 0, top)
    return jnp.take_along_axis(table, (jnp.arange(top)[None, :] + rotation) % top, axis=1)


def portions_of(count, total, bound, slope, full):
    loads = [(1 << 20) // math.isqrt(standing ** slope) + 1 for standing in range(1, count + 1)]
    largest = bound if full else min(bound, max(-(-total // count), total * loads[0] // sum(loads)))
    least = 1 if total - largest >= count - 1 else 0
    counts, spare = [largest] + [least] * (count - 1), total - largest - least * (count - 1)
    while spare > 0:
        candidates = [i for i in range(1, count) if counts[i] < largest] or [i for i in range(1, count) if counts[i] < bound]
        pool, left = sum([loads[i] for i in candidates]), spare
        for i in candidates:
            more = min(bound - counts[i], max(1, left * loads[i] // pool), spare)
            counts[i] = counts[i] + more
            spare = spare - more
    return np.array(counts)


def bell_draw(rng, dims, width, most, cuts=(), kind=jnp.bfloat16):
    result = jax.random.normal(rng, dims, jnp.float32) * width
    if len(cuts) > 0:
        result = steps_of(rng, dims, cuts, -0.22, 0.18) * result
    return jnp.clip(result, min=-most, max=most).astype(kind)


def setup_inputs(seed: int = 0) -> dict:
    streams_of = jax.random.split(jax.random.key(seed), 8)
    tokens = bell_draw(streams_of[0], (TOKENS, D), 1.0, 6.0, ((0, 64),))
    route_keys = jax.random.split(jax.random.fold_in(streams_of[1], 1), TOKENS // TOK_DEV)
    route_turns = jax.random.permutation(jax.random.fold_in(streams_of[1], 3), TOKENS // TOK_DEV)
    route = jax.vmap(lambda own, number: assign_block(jax.random.fold_in(streams_of[1], 2), own, number, TOK_DEV, EXPERTS, TOP, CAP, 2))(route_keys, route_turns).reshape((TOKENS, TOP))
    gate_code = set_ends(jax.random.randint(streams_of[2], (TOKENS, TOP), 1, 1000), jax.random.fold_in(streams_of[2], 1), 1, 999).astype(jnp.int32)
    cotangent = bell_draw(streams_of[3], (TOKENS, D), 1.0, 6.0, ((0, 64),))
    w_gate = bell_draw(streams_of[4], (EXPERTS, D, FF), D ** -0.5, 0.09375, ((0, 64), (2, 12)))
    w_up = bell_draw(streams_of[5], (EXPERTS, D, FF), D ** -0.5, 0.09375, ((0, 64), (2, 12)))
    w_down = bell_draw(streams_of[6], (EXPERTS, FF, D), FF ** -0.5, 0.15625, ((0, 64), (1, 12)))
    return dict(tokens=tokens, route=route, gate_code=gate_code, cotangent=cotangent, w_gate=w_gate, w_up=w_up, w_down=w_down)


def reference(tokens, route, gate_code, cotangent, w_gate, w_up, w_down):
    pair_total = TOKENS * TOP
    block_pairs = TOK_DEV * TOP
    slot_count = N_EXPERT * CAP
    codes = gate_code.astype(jnp.float32)
    gates = codes / jnp.sum(codes, axis=1, keepdims=True)
    flat_route = route.reshape(-1).astype(jnp.int32)
    onehot = (flat_route[:, None] == jnp.arange(EXPERTS, dtype=jnp.int32)[None, :]).astype(jnp.int32)
    blocks = onehot.reshape(N_EXPERT, block_pairs, EXPERTS)
    before = jnp.cumsum(blocks, axis=1) - blocks
    slot_rank = jnp.sum(before * blocks, axis=2).reshape(-1).astype(jnp.int32)
    pair_ids = jnp.arange(pair_total, dtype=jnp.int32)
    source = pair_ids // block_pairs
    column = (source * CAP + slot_rank).astype(jnp.int32)
    table = jnp.zeros((EXPERTS, slot_count), jnp.int32).at[flat_route, column].set(pair_ids + 1)
    token_of = pair_ids // TOP
    pair_rows = jnp.concatenate([jnp.zeros((1, D), jnp.bfloat16), tokens[token_of]], axis=0)
    pair_grad = (gates.reshape(-1)[:, None] * cotangent[token_of].astype(jnp.float32)).astype(jnp.bfloat16)
    pair_grad = jnp.concatenate([jnp.zeros((1, D), jnp.bfloat16), pair_grad], axis=0)

    def expert_step(items):
        index_row, weight_gate, weight_up, weight_down = items
        rows = pair_rows[index_row]
        grads = pair_grad[index_row]
        gate_pre = jnp.dot(rows, weight_gate, preferred_element_type=jnp.float32)
        up_pre = jnp.dot(rows, weight_up, preferred_element_type=jnp.float32)
        sigma = jax.nn.sigmoid(gate_pre)
        silu_gate = gate_pre * sigma
        hidden = (silu_gate * up_pre).astype(jnp.bfloat16)
        hidden_groups = hidden.reshape(slot_count, N_DP, FD).transpose(1, 0, 2).astype(jnp.float32)
        down_groups = weight_down.reshape(N_DP, FD, D).astype(jnp.float32)
        part_out = jnp.einsum('nsf,nfd->nsd', hidden_groups, down_groups).astype(jnp.bfloat16)
        expert_out = jnp.sum(part_out.astype(jnp.float32), axis=0)
        grad_hidden = jnp.dot(grads, weight_down.T, preferred_element_type=jnp.float32)
        grad_gate_pre = (grad_hidden * up_pre * sigma * (1.0 + gate_pre * (1.0 - sigma))).astype(jnp.bfloat16)
        grad_up_pre = (grad_hidden * silu_gate).astype(jnp.bfloat16)
        gg_groups = grad_gate_pre.reshape(slot_count, N_DP, FD).transpose(1, 0, 2).astype(jnp.float32)
        gu_groups = grad_up_pre.reshape(slot_count, N_DP, FD).transpose(1, 0, 2).astype(jnp.float32)
        wg_groups = weight_gate.reshape(D, N_DP, FD).transpose(1, 2, 0).astype(jnp.float32)
        wu_groups = weight_up.reshape(D, N_DP, FD).transpose(1, 2, 0).astype(jnp.float32)
        part_input = (jnp.einsum('nsf,nfd->nsd', gg_groups, wg_groups)
                      + jnp.einsum('nsf,nfd->nsd', gu_groups, wu_groups)).astype(jnp.bfloat16)
        input_sum = jnp.sum(part_input.astype(jnp.float32), axis=0)
        grad_weight = jnp.dot(hidden.T, grads, preferred_element_type=jnp.float32).astype(jnp.bfloat16)
        return expert_out, input_sum, grad_weight

    outs_all, inputs_all, grad_down = lax.map(expert_step, (table, w_gate, w_up, w_down))
    flat_index = table.reshape(-1)
    pair_out = jnp.zeros((pair_total + 1, D), jnp.float32).at[flat_index].add(outs_all.reshape(-1, D))[1:]
    pair_input = jnp.zeros((pair_total + 1, D), jnp.float32).at[flat_index].add(inputs_all.reshape(-1, D))[1:]
    out3 = pair_out.reshape(TOKENS, TOP, D)
    mixed = jnp.sum(gates[:, :, None] * out3, axis=1).astype(jnp.bfloat16)
    grad_gates = jnp.sum(cotangent.astype(jnp.float32)[:, None, :] * out3, axis=2)
    grad_tokens = jnp.sum(pair_input.reshape(TOKENS, TOP, D), axis=1).astype(jnp.bfloat16)
    return mixed, grad_tokens, grad_gates, grad_down
```

```python
import jax
import jax.numpy as jnp
from jax import lax
from jax.sharding import PartitionSpec as P


def local(tokens, route, gate_code, cotangent, w_gate, w_up, w_down):
    n_expert = lax.axis_size("expert")
    tok_rows, width = tokens.shape
    top_k = route.shape[1]
    capacity = min(tok_rows, max(2, 4 * tok_rows * top_k // (3 * n_expert)))
    slot_count = n_expert * capacity
    codes = gate_code.astype(jnp.float32)
    gates = codes / jnp.sum(codes, axis=1, keepdims=True)
    flat_route = route.reshape(-1)
    onehot = (flat_route[:, None] == jnp.arange(n_expert, dtype=jnp.int32)[None, :]).astype(
        jnp.int32
    )
    before = jnp.cumsum(onehot, axis=0) - onehot
    slot_rank = jnp.sum(before * onehot, axis=1)
    slot_index = flat_route * capacity + slot_rank
    placing = (slot_index[None, :] == jnp.arange(slot_count, dtype=jnp.int32)[:, None]).astype(
        jnp.bfloat16
    )
    token_pick = jnp.sum(placing.reshape(slot_count, tok_rows, top_k), axis=2)
    send_rows = jnp.dot(token_pick, tokens, preferred_element_type=jnp.float32).astype(jnp.bfloat16)
    pair_grad = (
        gates.reshape(-1)[:, None] * jnp.repeat(cotangent, top_k, axis=0).astype(jnp.float32)
    ).astype(jnp.bfloat16)
    send_grad = jnp.dot(placing, pair_grad, preferred_element_type=jnp.float32).astype(jnp.bfloat16)
    shape3 = (n_expert, capacity, width)
    recv_rows, recv_grad = (
        lax.all_to_all(
            send_rows.reshape(shape3), "expert", split_axis=0, concat_axis=0, tiled=True
        ),
        lax.all_to_all(
            send_grad.reshape(shape3), "expert", split_axis=0, concat_axis=0, tiled=True
        ),
    )
    recv_rows = recv_rows.reshape(slot_count, width)
    recv_grad = recv_grad.reshape(slot_count, width)
    weight_gate = w_gate[0]
    weight_up = w_up[0]
    weight_down = w_down[0]
    gate_pre = jnp.dot(recv_rows, weight_gate, preferred_element_type=jnp.float32)
    up_pre = jnp.dot(recv_rows, weight_up, preferred_element_type=jnp.float32)
    sigma = jax.nn.sigmoid(gate_pre)
    silu_gate = gate_pre * sigma
    hidden = (silu_gate * up_pre).astype(jnp.bfloat16)
    expert_out = jnp.dot(hidden, weight_down, preferred_element_type=jnp.float32).astype(
        jnp.bfloat16
    )
    grad_hidden = lax.dot_general(
        recv_grad, weight_down, (((1,), (1,)), ((), ())), preferred_element_type=jnp.float32
    )
    grad_gate_pre = (grad_hidden * up_pre * sigma * (1.0 + gate_pre * (1.0 - sigma))).astype(
        jnp.bfloat16
    )
    grad_up_pre = (grad_hidden * silu_gate).astype(jnp.bfloat16)
    input_part = (
        lax.dot_general(
            grad_gate_pre, weight_gate, (((1,), (1,)), ((), ())), preferred_element_type=jnp.float32
        )
        + lax.dot_general(
            grad_up_pre, weight_up, (((1,), (1,)), ((), ())), preferred_element_type=jnp.float32
        )
    ).astype(jnp.bfloat16)
    grad_weight = lax.dot_general(
        hidden, recv_grad, (((0,), (0,)), ((), ())), preferred_element_type=jnp.float32
    ).astype(jnp.bfloat16)
    cot_float = cotangent.astype(jnp.float32)
    back_out, back_input = (
        lax.all_to_all(
            expert_out.reshape(shape3), "expert", split_axis=0, concat_axis=0, tiled=True
        ),
        lax.all_to_all(
            input_part.reshape(shape3), "expert", split_axis=0, concat_axis=0, tiled=True
        ),
    )
    pair_out = lax.dot_general(
        placing,
        back_out.reshape(slot_count, width),
        (((0,), (0,)), ((), ())),
        preferred_element_type=jnp.float32,
    )
    pair_input = lax.dot_general(
        placing,
        back_input.reshape(slot_count, width),
        (((0,), (0,)), ((), ())),
        preferred_element_type=jnp.float32,
    )
    out3 = pair_out.reshape(tok_rows, top_k, width)
    mixed_part = jnp.sum(gates[:, :, None] * out3, axis=1).astype(jnp.bfloat16)
    gates_part = jnp.sum(cot_float[:, None, :] * out3, axis=2)
    tokens_part = jnp.sum(pair_input.reshape(tok_rows, top_k, width), axis=1).astype(jnp.bfloat16)
    mixed, grad_tokens, grad_gates = (
        lax.psum(mixed_part, "dp"),
        lax.psum(tokens_part, "dp"),
        lax.psum(gates_part, "dp"),
    )
    return mixed, grad_tokens, grad_gates, grad_weight[None]


def solution(mesh):
    return jax.shard_map(
        local,
        mesh=mesh,
        in_specs=(
            P("expert", None),
            P("expert", None),
            P("expert", None),
            P("expert", None),
            P("expert", None, "dp"),
            P("expert", None, "dp"),
            P("expert", "dp", None),
        ),
        out_specs=(
            P("expert", None),
            P("expert", None),
            P("expert", None),
            P("expert", "dp", None),
        ),
        check_vma=False,
    )
```

```python
import functools

import jax
import jax.numpy as jnp
from jax import lax
from jax.experimental import pallas as pl
from jax.experimental.pallas import tpu as pltpu
from jax.sharding import PartitionSpec as P

ROWS_Y = 8
CORES = 2
CAP = 2
LANE = 128
F32 = jnp.float32
BF16 = jnp.bfloat16
MESH = pl.DeviceIdType.MESH


def mm(a, b, ca=1, cb=0):
    return lax.dot_general(a, b, (((ca,), (cb,)), ((), ())), preferred_element_type=F32)


def when(cond, body):
    if cond is None:
        body()
    else:
        pl.when(cond)(body)


class Split:
    def __init__(self, n, tiles):
        self.n, self.tiles = n, tiles
        self.base, self.extra = tiles // n, tiles % n
        self.size = self.base + (1 if self.extra else 0)
        self.slots = 2 * self.size
        self.pieces = [(0, self.base, None)]
        if self.extra:
            self.pieces.append((self.base, 1, self.more_first))
        self.half = len(self.pieces)
        self.pieces.append((self.size, self.base, None))
        if self.extra:
            self.pieces.append((self.size + self.base, 1, self.more_second))

    def more_first(self, o):
        return o < self.extra

    def more_second(self, o):
        return o >= self.n - self.extra

    def first(self, o):
        return self.base * o + jnp.minimum(o, self.extra)

    def second(self, o):
        return self.base * o + jnp.maximum(o - (self.n - self.extra), 0)

    def static(self, o):
        a = self.base * o + min(o, self.extra)
        b = self.base * o + max(o - (self.n - self.extra), 0)
        na = self.base + (1 if o < self.extra else 0)
        nb = self.base + (1 if o >= self.n - self.extra and self.extra else 0)
        return [(j, 0, a + j) for j in range(na)] + [(self.size + j, 1, b + j) for j in range(nb)]


def iota(shape, axis):
    return lax.broadcasted_iota(jnp.int32, shape, axis)


def kernel(
    n, n_expert,
    route, codes, tokens, cot, wg, wu, wd,
    mixed, gtok, ggates, gdown,
    wgu, wdv, gdv, snd1, rcv1, snd2, gall, pre, ghid, part, hid, hidt, ggu,
    sndl, rcvl, sndr, rcvr, ybuf, rcv3, snd4, rcv4, fin, gfin,
    wsem, s1, r1, s2, r2, gs, gr, ls, lr, rs, rr, s3, r3, s4, r4, fs, fr, osem,
):
    ny = ROWS_Y
    a_n = n_expert // ny
    rows_y, rows_a = a_n * CAP, ny * CAP
    slots = n_expert * CAP
    top, tok_n = route.shape
    width = tokens.shape[1]
    tiles = width // LANE
    sp = Split(n, tiles)
    size, chunk_w = sp.size, sp.size * LANE
    r_max, l_max = n // 2, (n - 1) // 2

    z = lax.axis_index("dp")
    e = lax.axis_index("expert")
    core = lax.rem(e, CORES)
    y = lax.rem(e // CORES, ny)
    x = e // (CORES * ny)
    xc = x * CORES + core
    right, left = lax.rem(z + 1, n), lax.rem(z + n - 1, n)

    def y_peer(i):
        yp = lax.rem(y + i, ny)
        return yp, (z, (x * ny + yp) * CORES + core)

    def a_peer(i):
        ap = lax.rem(xc + i, a_n)
        return ap, (z, ((ap // CORES) * ny + y) * CORES + lax.rem(ap, CORES))

    def copy(src, dst, ssem, rsem, device):
        return pltpu.make_async_remote_copy(
            src_ref=src, dst_ref=dst, send_sem=ssem, recv_sem=rsem, device_id=device, device_id_type=MESH
        )

    f = wdv.shape[0]
    loads = [
        pltpu.make_async_copy(wg, wgu.at[pl.ds(0, width), pl.ds(0, f)], wsem.at[0]),
        pltpu.make_async_copy(wu, wgu.at[pl.ds(0, width), pl.ds(f, f)], wsem.at[1]),
        pltpu.make_async_copy(wd, wdv, wsem.at[2]),
    ]
    for load in loads:
        load.start()
    if sp.extra:
        wgu[pl.ds(width, LANE), :] = jnp.zeros((LANE, 2 * f), BF16)
        for o in range(n):
            held = {slot for slot, _, _ in sp.static(o)}
            for j in range(sp.slots):
                if j not in held:
                    gall[o, j] = jnp.zeros((slots, LANE), BF16)
    pre[...] = jnp.zeros_like(pre)
    ghid[...] = jnp.zeros_like(ghid)

    barrier = pltpu.get_barrier_semaphore()
    peers = [y_peer(i)[1] for i in range(1, ny)] + [a_peer(i)[1] for i in range(1, a_n)]
    peers += [(right, e), (left, e)]
    for peer in peers:
        pl.semaphore_signal(barrier, inc=1, device_id=peer, device_id_type=MESH)

    s_id = iota((slots, tok_n), 0)
    s_xc = (s_id // CAP) % a_n
    s_expert = ((s_xc // CORES) * ny + s_id // rows_y) * CORES + s_xc % CORES
    s_rank = (s_id % CAP).astype(F32)
    code_f = codes[...].astype(F32)
    gates = code_f / jnp.sum(code_f, axis=0, keepdims=True)
    hits = [route[k:k + 1, :] == s_expert for k in range(top)]
    named = jnp.zeros((slots, tok_n), F32)
    gate_of = jnp.zeros((slots, tok_n), F32)
    for k in range(top):
        named = named + jnp.where(hits[k], 1.0, 0.0)
        gate_of = gate_of + jnp.where(hits[k], gates[k:k + 1, :], 0.0)
    earlier = jnp.where(iota((tok_n, tok_n), 0) < iota((tok_n, tok_n), 1), 1.0, 0.0).astype(BF16)
    before = mm(named.astype(BF16), earlier)
    pick_f = jnp.where(before == s_rank, named, 0.0)
    pick = pick_f.astype(BF16)
    gate_of = gate_of * pick_f
    gate = jnp.sum(gate_of, axis=1, keepdims=True)

    def own_columns(ref, start, more):
        parts = []
        for j in range(size):
            at = jnp.minimum(start + j, tiles - 1)
            block = ref[:, pl.ds(pl.multiple_of(at * LANE, LANE), LANE)]
            if j >= sp.base:
                block = jnp.where(more(z), block, jnp.zeros_like(block))
            parts.append(block)
        return jnp.concatenate(parts, axis=1)

    def split_store(ref, slot0, value, groups):
        for j in range(value.shape[1] // LANE):
            ref[:, slot0 + j] = value[:, j * LANE:(j + 1) * LANE].reshape(groups, slots // groups, LANE)

    split_store(snd1, 0, mm(pick, own_columns(tokens, sp.first(z), sp.more_first)).astype(BF16), ny)
    cot_rows = mm(pick, own_columns(cot, sp.second(z), sp.more_second))
    split_store(snd1, size, (cot_rows * gate).astype(BF16), ny)

    pl.semaphore_wait(barrier, len(peers))

    def along_y(src, dst, ssem, rsem):
        copies = []
        for i in range(1, ny):
            yp, device = y_peer(i)
            copies.append(copy(src.at[yp], dst.at[y], ssem.at[i], rsem.at[i], device))
        for c in copies:
            c.start()
        dst[y] = src[y]
        for c in copies:
            c.wait_recv()
        return copies

    def regroup(src, outer, inner):
        to, at = iota((slots, slots), 0), iota((slots, slots), 1)
        want = ((to // CAP) % outer) * (inner * CAP) + (to // (outer * CAP)) * CAP + to % CAP
        move = jnp.where(at == want, 1.0, 0.0).astype(BF16)
        whole = jnp.concatenate([src[:, j].reshape(slots, LANE) for j in range(sp.slots)], axis=1)
        return mm(move, whole).astype(BF16)

    sends = along_y(snd1, rcv1, s1, r1)
    split_store(snd2, 0, regroup(rcv1, ny, a_n), a_n)
    copies = []
    rows = pl.ds(pl.multiple_of(xc * rows_a, rows_a), rows_a)
    for i in range(1, a_n):
        ap, device = a_peer(i)
        copies.append(copy(snd2.at[ap], gall.at[z, :, rows], s2.at[i], r2.at[i], device))
    for c in copies:
        c.start()
    for j in range(sp.slots):
        gall[z, j, rows] = snd2[xc, j]
    for c in copies:
        c.wait_recv()
    sends += copies

    def to_right(d):
        return lax.rem(z + n - d, n), (right, e)

    def to_left(d):
        return lax.rem(z + d, n), (left, e)

    ways = ((to_right, r_max), (to_left, l_max))

    def gather_copy(way, d, p):
        o, device = ways[way][0](d)
        at, count, cond = sp.pieces[p]
        block = gall.at[o, pl.ds(at, count)]
        return copy(block, block, gs.at[way, d, p], gr.at[way, d + 1, p], device), cond and cond(o)

    def gather_arrival(way, d, p):
        o, device = ways[way][0](d)
        at, count, cond = sp.pieces[p]
        block = gall.at[o, pl.ds(at, count)]
        return copy(block, block, gs.at[way, d, p], gr.at[way, d, p], device), cond and cond(o)

    def use_first(o):
        block = jnp.concatenate([gall[o, j] for j in range(size)], axis=1)
        at = pl.multiple_of(sp.first(o) * LANE, LANE)
        pre[...] += mm(block, wgu[pl.ds(at, chunk_w), :])

    def use_second(o):
        block = jnp.concatenate([gall[o, size + j] for j in range(size)], axis=1)
        at = pl.multiple_of(sp.second(o) * LANE, LANE)
        ghid[...] += mm(block, wdv[:, pl.ds(at, chunk_w)], 1, 1)

    def gather_step(d, forwards):
        for ps, use in ((range(sp.half), use_first), (range(sp.half, len(sp.pieces)), use_second)):
            for way in range(2):
                if forwards[way] is None:
                    continue
                for p in ps:
                    arrival, cond = gather_arrival(way, d, p)

                    def on(arrival=arrival, way=way, p=p):
                        arrival.wait_recv()
                        if forwards[way]:
                            gather_copy(way, d, p)[0].start()

                    when(cond, on)
            for way in range(2):
                if forwards[way] is not None:
                    use(ways[way][0](d)[0])

    for p in range(len(sp.pieces)):
        for way in range(2):
            c, cond = gather_copy(way, 0, p)
            when(cond, c.start)
    for load in loads:
        load.wait()
    use_first(z)
    use_second(z)

    def gather_body(d, carry):
        gather_step(d, (True, True))
        return carry

    lax.fori_loop(1, l_max, gather_body, 0)
    gather_step(l_max, (r_max > l_max, False))
    if r_max > l_max:
        gather_step(r_max, (False, None))

    gate_pre, up_pre, grad_hidden = pre[:, :f], pre[:, f:], ghid[...]
    sigma = 1.0 / (1.0 + jnp.exp(-gate_pre))
    silu = gate_pre * sigma
    hidden = silu * up_pre
    hid[...] = hidden.astype(BF16)
    hidt[...] = hidden.T.astype(BF16)
    ggu[:, :f] = (grad_hidden * up_pre * sigma * (1.0 + gate_pre * (1.0 - sigma))).astype(BF16)
    ggu[:, f:] = (grad_hidden * silu).astype(BF16)

    def make_part(which, o):
        at = pl.multiple_of(sp.first(o) * LANE, LANE)
        value = mm(ggu[...], wgu[pl.ds(at, chunk_w), :], 1, 1)
        for j in range(size):
            part[which, j] = value[:, j * LANE:(j + 1) * LANE]
        at = pl.multiple_of(sp.second(o) * LANE, LANE)
        value = mm(hid[...], wdv[:, pl.ds(at, chunk_w)])
        for j in range(size):
            part[which, size + j] = value[:, j * LANE:(j + 1) * LANE]

    flows = ((sndl, rcvl, ls, lr, to_right, (left, e)), (sndr, rcvr, rs, rr, to_left, (right, e)))

    def scatter_copy(flow, d, p):
        snd, rcv, ssem, rsem, owner, device = flows[flow]
        at, count, cond = sp.pieces[p]
        c = copy(snd.at[d, pl.ds(at, count)], rcv.at[d - 1, pl.ds(at, count)], ssem.at[d, p], rsem.at[d - 1, p], device)
        return c, cond and cond(owner(d)[0])

    def scatter_arrival(flow, d, p):
        snd, rcv, ssem, rsem, owner, device = flows[flow]
        at, count, cond = sp.pieces[p]
        c = copy(rcv.at[d, pl.ds(at, count)], rcv.at[d, pl.ds(at, count)], ssem.at[0, p], rsem.at[d, p], device)
        return c, cond and cond(owner(d)[0])

    def scatter_first(flow, d):
        snd = flows[flow][0]
        make_part(flow, flows[flow][4](d)[0])
        for p, (at, count, _) in enumerate(sp.pieces):
            c, cond = scatter_copy(flow, d, p)

            def on(c=c, at=at, count=count):
                snd[d, pl.ds(at, count)] = part[flow, pl.ds(at, count)].astype(BF16)
                c.start()

            when(cond, on)

    def scatter_step(flow_d):
        for flow, d in flow_d:
            make_part(flow, flows[flow][4](d)[0])
        for p, (at, count, _) in enumerate(sp.pieces):
            for flow, d in flow_d:
                snd, rcv = flows[flow][:2]
                arrival, cond = scatter_arrival(flow, d, p)

                def on(flow=flow, d=d, snd=snd, rcv=rcv, arrival=arrival):
                    arrival.wait_recv()
                    total = part[flow, pl.ds(at, count)] + rcv[d, pl.ds(at, count)].astype(F32)
                    snd[d, pl.ds(at, count)] = total.astype(BF16)
                    scatter_copy(flow, d, p)[0].start()

                when(cond, on)

    def make_gdown(o):
        block = jnp.concatenate([gall[o, size + j] for j in range(size)], axis=1)
        at = pl.multiple_of(sp.second(o) * LANE, LANE)
        gdv[:, pl.ds(at, chunk_w)] = mm(hidt[...], block).astype(BF16)

    scatter_first(0, r_max)
    scatter_first(1, l_max)

    def scatter_body(i, carry):
        scatter_step(((0, r_max - i), (1, l_max - i)))
        return carry

    lax.fori_loop(1, l_max, scatter_body, 0)
    if r_max > l_max:
        scatter_step(((0, 1),))

    def gdown_body(o, carry):
        make_gdown(o)
        return carry

    lax.fori_loop(0, n, gdown_body, 0)
    store = pltpu.make_async_copy(gdv, gdown, osem)
    store.start()

    make_part(0, z)
    for p, (at, count, _) in enumerate(sp.pieces):
        block = pl.ds(at, count)
        cond = None
        for flow in range(2):
            arrival, cond = scatter_arrival(flow, 0, p)
            when(cond, arrival.wait_recv)

        def on(block=block):
            total = part[0, block] + rcvl[0, block].astype(F32) + rcvr[0, block].astype(F32)
            ybuf[block] = total.astype(BF16)

        if cond is not None:
            ybuf[block] = jnp.zeros_like(ybuf[block])
        when(cond, on)

    copies = []
    for i in range(1, a_n):
        ap, device = a_peer(i)
        to = pl.ds(pl.multiple_of(ap * rows_a, rows_a), rows_a)
        copies.append(copy(ybuf.at[:, to], rcv3.at[xc], s3.at[i], r3.at[i], device))
    for c in copies:
        c.start()
    for j in range(sp.slots):
        rcv3[xc, j] = ybuf[j, rows]
    for c in copies:
        c.wait_recv()
    sends += copies
    split_store(snd4, 0, regroup(rcv3, a_n, ny), ny)
    sends += along_y(snd4, rcv4, s4, r4)

    back = [rcv4[:, j].reshape(slots, LANE) for j in range(sp.slots)]
    back_in, back_out = jnp.concatenate(back[:size], axis=1), jnp.concatenate(back[size:], axis=1)
    eye = jnp.where(iota((tok_n, tok_n), 0) == iota((tok_n, tok_n), 1), 1.0, 0.0).astype(BF16)
    high = gate_of.astype(BF16)
    low = (gate_of - high.astype(F32)).astype(BF16)
    high_t, low_t, pick_t = [mm(eye, v, 1, 1).astype(BF16) for v in (high, low, pick)]
    mixed_part = (mm(high_t, back_out) + mm(low_t, back_out)).astype(BF16)
    gtok_part = mm(pick_t, back_in).astype(BF16)
    for j in range(size):
        fin[z, j] = gtok_part[:, j * LANE:(j + 1) * LANE]
        fin[z, size + j] = mixed_part[:, j * LANE:(j + 1) * LANE]
    inner = mm(back_out, own_columns(cot, sp.second(z), sp.more_second), 1, 1) * pick_f
    gfin[z] = jnp.zeros(gfin.shape[1:], F32)
    for k in range(top):
        gfin[z, k:k + 1, 0:tok_n] = jnp.sum(jnp.where(hits[k], inner, 0.0), axis=0, keepdims=True)

    def final_copy(way, d, which, arrival):
        o, device = ways[way][0](d)
        ref = (fin, gfin)[which]
        return copy(ref.at[o], ref.at[o], fs.at[way, d, which], fr.at[way, d + (0 if arrival else 1), which], device)

    def final_step(d, forwards):
        for which in range(2):
            for way in range(2):
                if forwards[way] is None:
                    continue
                final_copy(way, d, which, True).wait_recv()
                if forwards[way]:
                    final_copy(way, d, which, False).start()

    for which in range(2):
        for way in range(2):
            final_copy(way, 0, which, False).start()

    def final_body(d, carry):
        final_step(d, (True, True))
        return carry

    lax.fori_loop(1, l_max, final_body, 0)
    final_step(l_max, (r_max > l_max, False))
    if r_max > l_max:
        final_step(r_max, (False, None))

    total = jnp.zeros(gfin.shape[1:], F32)
    for o in range(n):
        total = total + gfin[o]
        for slot, which, tile in sp.static(o):
            (gtok, mixed)[which][:, tile * LANE:(tile + 1) * LANE] = fin[o, slot]
    ggates[...] = total[:, 0:tok_n]

    for c in sends:
        c.wait_send()
    for way in range(2):

        def done(d, carry, way=way):
            for p in range(len(sp.pieces)):
                c, cond = gather_copy(way, d, p)
                when(cond, c.wait_send)
                c, cond = scatter_copy(way, d + 1, p)
                when(cond, c.wait_send)
            for which in range(2):
                final_copy(way, d, which, False).wait_send()
            return carry

        lax.fori_loop(0, (r_max, l_max)[way], done, 0)
    store.wait()


def local(n, n_expert, tokens, route, gate_code, cotangent, w_gate, w_up, w_down):
    tok_n, width = tokens.shape
    top = route.shape[1]
    f = w_gate.shape[2]
    ny, a_n = ROWS_Y, n_expert // ROWS_Y
    slots = n_expert * CAP
    sp = Split(n, width // LANE)
    k, np_ = sp.slots, len(sp.pieces)
    r_max, l_max = n // 2, (n - 1) // 2
    vmem = pl.BlockSpec(memory_space=pltpu.VMEM)
    anyw = pl.BlockSpec(memory_space=pl.ANY)
    dma = pltpu.SemaphoreType.DMA

    def b16(*shape):
        return pltpu.VMEM(shape, BF16)

    def f32(*shape):
        return pltpu.VMEM(shape, F32)

    rows_y, rows_a = a_n * CAP, ny * CAP
    mixed, gtok, ggates, gdown = pl.pallas_call(
        functools.partial(kernel, n, n_expert),
        out_shape=(
            jax.ShapeDtypeStruct((tok_n, width), BF16),
            jax.ShapeDtypeStruct((tok_n, width), BF16),
            jax.ShapeDtypeStruct((top, tok_n), F32),
            jax.ShapeDtypeStruct((f, width), BF16),
        ),
        in_specs=[vmem] * 4 + [anyw] * 3,
        out_specs=(vmem, vmem, vmem, anyw),
        scratch_shapes=[
            b16(width + (LANE if sp.extra else 0), 2 * f), b16(f, width), b16(f, width),
            b16(ny, k, rows_y, LANE), b16(ny, k, rows_y, LANE), b16(a_n, k, rows_a, LANE),
            b16(n, k, slots, LANE), f32(slots, 2 * f), f32(slots, f), f32(2, k, slots, LANE),
            b16(slots, f), b16(f, slots), b16(slots, 2 * f),
            b16(r_max + 1, k, slots, LANE), b16(r_max, k, slots, LANE),
            b16(l_max + 1, k, slots, LANE), b16(l_max, k, slots, LANE),
            b16(k, slots, LANE), b16(a_n, k, rows_a, LANE),
            b16(ny, k, rows_y, LANE), b16(ny, k, rows_y, LANE),
            b16(n, k, tok_n, LANE), f32(n, top, LANE),
            dma((3,)), dma((ny,)), dma((ny,)), dma((a_n,)), dma((a_n,)),
            dma((2, r_max, np_)), dma((2, r_max + 1, np_)),
            dma((r_max + 1, np_)), dma((r_max, np_)), dma((l_max + 1, np_)), dma((l_max, np_)),
            dma((a_n,)), dma((a_n,)), dma((ny,)), dma((ny,)),
            dma((2, r_max, 2)), dma((2, r_max + 1, 2)), dma,
        ],
        compiler_params=pltpu.CompilerParams(
            collective_id=0, has_side_effects=True, vmem_limit_bytes=48 * 1024 * 1024
        ),
        name="moe_step",
    )(route.T, gate_code.T, tokens, cotangent, w_gate[0], w_up[0], w_down[0])
    return mixed, gtok, ggates.T, gdown[None]


def solution(mesh):
    n, n_expert = mesh.shape["dp"], mesh.shape["expert"]
    return jax.shard_map(
        functools.partial(local, n, n_expert),
        mesh=mesh,
        in_specs=(
            P("expert", None),
            P("expert", None),
            P("expert", None),
            P("expert", None),
            P("expert", None, "dp"),
            P("expert", None, "dp"),
            P("expert", "dp", None),
        ),
        out_specs=(
            P("expert", None),
            P("expert", None),
            P("expert", None),
            P("expert", "dp", None),
        ),
        check_vma=False,
    )
```

```python
import functools

import jax
import jax.numpy as jnp
from jax import lax
from jax.experimental import pallas as pl
from jax.experimental.pallas import tpu as pltpu
from jax.sharding import PartitionSpec as P

ROWS_Y = 8
CORES = 2
CAP = 2
LANE = 128
F32 = jnp.float32
BF16 = jnp.bfloat16
MESH = pl.DeviceIdType.MESH
DIRECT = 12
GROUPS = 2


def mm(a, b, ca=1, cb=0):
    return lax.dot_general(a, b, (((ca,), (cb,)), ((), ())), preferred_element_type=F32)


def when(cond, body):
    if cond is None:
        body()
    else:
        pl.when(cond)(body)


class Split:
    def __init__(self, n, tiles):
        self.n, self.tiles = n, tiles
        self.base, self.extra = tiles // n, tiles % n
        self.size = self.base + (1 if self.extra else 0)
        self.slots = 2 * self.size
        self.pieces = [(0, self.base, None)]
        if self.extra:
            self.pieces.append((self.base, 1, self.more_first))
        self.half = len(self.pieces)
        self.pieces.append((self.size, self.base, None))
        if self.extra:
            self.pieces.append((self.size + self.base, 1, self.more_second))

    def more_first(self, o):
        return o < self.extra

    def more_second(self, o):
        return o >= self.n - self.extra

    def first(self, o):
        return self.base * o + jnp.minimum(o, self.extra)

    def second(self, o):
        return self.base * o + jnp.maximum(o - (self.n - self.extra), 0)

    def group(self, p):
        return 0 if p < self.half else 1

    def static(self, o):
        a = self.base * o + min(o, self.extra)
        b = self.base * o + max(o - (self.n - self.extra), 0)
        na = self.base + (1 if o < self.extra else 0)
        nb = self.base + (1 if o >= self.n - self.extra and self.extra else 0)
        return [(j, 0, a + j) for j in range(na)] + [(self.size + j, 1, b + j) for j in range(nb)]


def iota(shape, axis):
    return lax.broadcasted_iota(jnp.int32, shape, axis)


def kernel(
    n, n_expert,
    route_h, codes_h, tokens_h, cot_h, wg, wu, wd,
    mixed, gtok, ggates, gdown,
    route, codes, tokens, cot, wgu, wdv, gdv, snd1, rcv1, snd2, gall, snd1d, rcv1d, snd2d, gdir, pre, ghid, part, hid, hidt, ggu,
    sndl, rcvl, sndr, rcvr, ybuf, snd3, rcv3, snd4, rcv4, fin, gfin,
    isem, wsem, s1, r1, s2, r2, s1d, r1d, s2d, r2d, gs, gr, ls, lr, rs, rr, s3, r3, s4, r4, fs, fr, osem,
):
    ny = ROWS_Y
    a_n = n_expert // ny
    rows_y, rows_a = a_n * CAP, ny * CAP
    slots = n_expert * CAP
    top, tok_n = route.shape
    width = tokens.shape[1]
    tiles = width // LANE
    direct = DIRECT if tiles > DIRECT else 0
    ringed = tiles - direct
    per = direct // GROUPS
    sd, sp = Split(n, ringed), Split(n, tiles)
    size, chunk_w = sp.size, sp.size * LANE
    hops = n // 2
    shared = n % 2 == 0

    def travels(hop, way, group):
        return hop < hops or (hop == hops and (not shared or way == group))

    z = lax.axis_index("dp")
    e = lax.axis_index("expert")
    core = lax.rem(e, CORES)
    y = lax.rem(e // CORES, ny)
    x = e // (CORES * ny)
    xc = x * CORES + core
    right, left = lax.rem(z + 1, n), lax.rem(z + n - 1, n)

    def y_peer(i):
        yp = lax.rem(y + i, ny)
        return yp, (z, (x * ny + yp) * CORES + core)

    def a_peer(i):
        ap = lax.rem(xc + i, a_n)
        return ap, (z, ((ap // CORES) * ny + y) * CORES + lax.rem(ap, CORES))

    def copy(src, dst, ssem, rsem, device):
        return pltpu.make_async_remote_copy(
            src_ref=src, dst_ref=dst, send_sem=ssem, recv_sem=rsem, device_id=device, device_id_type=MESH
        )

    for o in range(n):
        held = {slot for slot, _, _ in sd.static(o)}
        for j in range(sd.slots):
            if j not in held:
                gall[o, j] = jnp.zeros((slots, LANE), BF16)
    if sp.extra or sd.extra:
        wgu[pl.ds(width, LANE), :] = jnp.zeros((LANE, wgu.shape[1]), BF16)

    barrier = pltpu.get_barrier_semaphore()
    peers = [y_peer(i)[1] for i in range(1, ny)] + [a_peer(i)[1] for i in range(1, a_n)]
    peers += [(lax.rem(z + i, n), e) for i in range(1, n)]
    for peer in peers:
        pl.semaphore_signal(barrier, inc=1, device_id=peer, device_id_type=MESH)

    f = wdv.shape[0]
    inputs = [
        pltpu.make_async_copy(src, dst, isem.at[i])
        for i, (src, dst) in enumerate(((route_h, route), (codes_h, codes), (tokens_h, tokens), (cot_h, cot)))
    ]
    loads = [
        pltpu.make_async_copy(wg, wgu.at[pl.ds(0, width), pl.ds(0, f)], wsem.at[0]),
        pltpu.make_async_copy(wu, wgu.at[pl.ds(0, width), pl.ds(f, f)], wsem.at[1]),
        pltpu.make_async_copy(wd, wdv, wsem.at[2]),
    ]
    for load in inputs + loads:
        load.start()
    pre[...] = jnp.zeros_like(pre)
    ghid[...] = jnp.zeros_like(ghid)
    for load in inputs:
        load.wait()

    code_f = codes[...].astype(F32)
    gates = code_f / jnp.sum(code_f, axis=0, keepdims=True)
    earlier = jnp.where(iota((tok_n, tok_n), 0) < iota((tok_n, tok_n), 1), 1.0, 0.0).astype(BF16)

    def slots_of(s_y, s_xc):
        s_expert = ((s_xc // CORES) * ny + s_y) * CORES + s_xc % CORES
        hits = [route[k:k + 1, :] == s_expert for k in range(top)]
        named = jnp.zeros((slots, tok_n), F32)
        gate_of = jnp.zeros((slots, tok_n), F32)
        for k in range(top):
            named = named + jnp.where(hits[k], 1.0, 0.0)
            gate_of = gate_of + jnp.where(hits[k], gates[k:k + 1, :], 0.0)
        before = mm(named.astype(BF16), earlier)
        pick_f = jnp.where(before == (s_id % CAP).astype(F32), named, 0.0)
        gate_of = gate_of * pick_f
        return hits, pick_f, gate_of, jnp.sum(gate_of, axis=1, keepdims=True)

    s_id = iota((slots, tok_n), 0)
    hits, pick_f, gate_of, gate = by_y = slots_of(s_id // rows_y, (s_id // CAP) % a_n)
    pick = pick_f.astype(BF16)

    def own_columns(split, ref, start, more):
        parts = []
        for j in range(split.size):
            at = jnp.minimum(start + j, tiles - 1)
            block = ref[:, pl.ds(pl.multiple_of(at * LANE, LANE), LANE)]
            if j >= split.base:
                block = jnp.where(more(z), block, jnp.zeros_like(block))
            parts.append(block)
        return jnp.concatenate(parts, axis=1)

    def split_store(ref, slot0, value, groups):
        for j in range(value.shape[1] // LANE):
            ref[:, slot0 + j] = value[:, j * LANE:(j + 1) * LANE].reshape(groups, slots // groups, LANE)

    def pick_first(order, columns):
        return mm(order[1].astype(BF16), columns).astype(BF16)

    def pick_second(order, columns):
        return (mm(order[1].astype(BF16), columns) * order[3]).astype(BF16)

    split_store(snd1, 0, pick_first(by_y, own_columns(sd, tokens, sd.first(z), sd.more_first)), ny)
    split_store(snd1, sd.size, pick_second(by_y, own_columns(sd, cot, sd.second(z), sd.more_second)), ny)

    pl.semaphore_wait(barrier, len(peers))

    sends = []
    axes = {"y": (y_peer, ny, y), "a": (a_peer, a_n, xc)}

    def exchange(axis, src, dst, ssem, rsem, by_rows=False):
        peer, count, me = axes[axis]
        height = slots // count
        rows = pl.ds(pl.multiple_of(me * height, height), height)
        to = dst.at[:, rows] if by_rows else dst.at[me]
        copies = []
        for i in range(1, count):
            b, device = peer(i)
            copies.append(copy(src.at[b], to, ssem.at[i], rsem.at[i], device))
        for c in copies:
            c.start()
        if by_rows:
            for j in range(src.shape[1]):
                dst[j, rows] = src[me, j]
        else:
            dst[me] = src[me]
        sends.extend(copies)
        return copies

    def arrive(copies):
        for c in copies:
            c.wait_recv()

    def permute(whole, outer, inner):
        to, at = iota((slots, slots), 0), iota((slots, slots), 1)
        want = ((to // CAP) % outer) * (inner * CAP) + (to // (outer * CAP)) * CAP + to % CAP
        move = jnp.where(at == want, 1.0, 0.0).astype(BF16)
        return mm(move, whole).astype(BF16)

    def regroup(src, outer, inner):
        whole = jnp.concatenate([src[:, j].reshape(slots, LANE) for j in range(src.shape[1])], axis=1)
        return permute(whole, outer, inner)

    def build(g, order, groups):
        at = (ringed + g * per) * LANE
        split_store(snd1d.at[g], 0, pick_first(order, tokens[:, at:at + per * LANE]), groups)
        split_store(snd1d.at[g], per, pick_second(order, cot[:, at:at + per * LANE]), groups)

    own = exchange("y", snd1, rcv1, s1, r1)
    if direct:
        build(1, slots_of((s_id // CAP) % ny, s_id // rows_a), a_n)
        second = exchange("a", snd1d.at[1], rcv1d.at[1], s1d.at[1], r1d.at[1])
    arrive(own)
    split_store(snd2, 0, regroup(rcv1, ny, a_n), a_n)
    own = exchange("a", snd2, gall.at[z], s2, r2, True)
    if direct:
        build(0, by_y, ny)
        first = exchange("y", snd1d.at[0], rcv1d.at[0], s1d.at[0], r1d.at[0])
        arrive(second)
        split_store(snd2d.at[1], 0, regroup(rcv1d.at[1], a_n, ny), ny)
        second = exchange("y", snd2d.at[1], gdir.at[1], s2d.at[1], r2d.at[1], True)
    arrive(own)

    def first_turn():
        arrive(first)
        split_store(snd2d.at[0], 0, regroup(rcv1d.at[0], ny, a_n), a_n)
        return exchange("a", snd2d.at[0], gdir.at[0], s2d.at[0], r2d.at[0], True)

    def direct_use(g):
        at = (ringed + g * per) * LANE
        block = jnp.concatenate([gdir[g, j] for j in range(per)], axis=1)
        pre[...] += mm(block, wgu[at:at + per * LANE, :])
        block = jnp.concatenate([gdir[g, per + j] for j in range(per)], axis=1)
        ghid[...] += mm(block, wdv[:, at:at + per * LANE], 1, 1)

    def to_right(d):
        return lax.rem(z + n - d, n), (right, e)

    def to_left(d):
        return lax.rem(z + d, n), (left, e)

    ways = (to_right, to_left)

    def gather_copy(way, d, p, arrival=False):
        o, device = ways[way](d)
        at, count, cond = sd.pieces[p]
        block = gall.at[o, pl.ds(at, count)]
        to = d if arrival else d + 1
        return copy(block, block, gs.at[way, d, p], gr.at[way, to, p], device), cond and cond(o)

    def use_first(o):
        block = jnp.concatenate([gall[o, j] for j in range(sd.size)], axis=1)
        at = pl.multiple_of(sd.first(o) * LANE, LANE)
        pre[...] += mm(block, wgu[pl.ds(at, sd.size * LANE), :])

    def use_second(o):
        block = jnp.concatenate([gall[o, sd.size + j] for j in range(sd.size)], axis=1)
        at = pl.multiple_of(sd.second(o) * LANE, LANE)
        ghid[...] += mm(block, wdv[:, pl.ds(at, sd.size * LANE)], 1, 1)

    def gather_step(d):
        for group, use in ((0, use_first), (1, use_second)):
            for p in range(len(sd.pieces)):
                if sd.group(p) != group:
                    continue
                for way in range(2):
                    if not travels(d, way, group):
                        continue
                    came, cond = gather_copy(way, d, p, True)

                    def on(came=came, way=way, p=p, group=group):
                        came.wait_recv()
                        if travels(d + 1, way, group):
                            gather_copy(way, d, p)[0].start()

                    when(cond, on)
            for way in range(2):
                if travels(d, way, group):
                    use(ways[way](d)[0])

    for p in range(len(sd.pieces)):
        for way in range(2):
            if travels(1, way, sd.group(p)):
                c, cond = gather_copy(way, 0, p)
                when(cond, c.start)
    for load in loads:
        load.wait()
    use_first(z)
    use_second(z)
    for d in range(1, hops + 1):
        gather_step(d)
        if direct and d == max(1, hops - 3):
            first = first_turn()
    if direct:
        arrive(second)
        whole = jnp.concatenate([gdir[1, j] for j in range(2 * per)], axis=1)
        whole = permute(whole, ny, a_n)
        for j in range(2 * per):
            gdir[1, j] = whole[:, j * LANE:(j + 1) * LANE]
        direct_use(1)
        arrive(first)
        direct_use(0)

    gate_pre, up_pre, grad_hidden = pre[:, :f], pre[:, f:], ghid[...]
    sigma = 1.0 / (1.0 + jnp.exp(-gate_pre))
    silu = gate_pre * sigma
    hidden = silu * up_pre
    hid[...] = hidden.astype(BF16)
    hidt[...] = hidden.T.astype(BF16)
    ggu[:, :f] = (grad_hidden * up_pre * sigma * (1.0 + gate_pre * (1.0 - sigma))).astype(BF16)
    ggu[:, f:] = (grad_hidden * silu).astype(BF16)

    def make_part(which, o, group):
        if group == 0:
            at = pl.multiple_of(sp.first(o) * LANE, LANE)
            value = mm(ggu[...], wgu[pl.ds(at, chunk_w), :], 1, 1)
        else:
            at = pl.multiple_of(sp.second(o) * LANE, LANE)
            value = mm(hid[...], wdv[:, pl.ds(at, chunk_w)])
        for j in range(size):
            part[which, group * size + j] = value[:, j * LANE:(j + 1) * LANE]

    flows = ((sndl, rcvl, ls, lr, to_right, (left, e)), (sndr, rcvr, rs, rr, to_left, (right, e)))

    def scatter_copy(flow, d, p, arrival=False):
        snd, rcv, ssem, rsem, owner, device = flows[flow]
        at, count, cond = sp.pieces[p]
        to = d if arrival else d - 1
        c = copy(snd.at[d, pl.ds(at, count)], rcv.at[to, pl.ds(at, count)], ssem.at[d, p], rsem.at[to, p], device)
        return c, cond and cond(owner(d)[0])

    def scatter_step(d):
        for flow in range(2):
            for group in range(2):
                if travels(d, flow, group):
                    make_part(flow, flows[flow][4](d)[0], group)
        for p, (at, count, _) in enumerate(sp.pieces):
            for flow in range(2):
                if not travels(d, flow, sp.group(p)):
                    continue
                snd, rcv = flows[flow][:2]
                going, cond = scatter_copy(flow, d, p)

                def on(flow=flow, snd=snd, rcv=rcv, going=going, p=p, at=at, count=count):
                    total = part[flow, pl.ds(at, count)]
                    if travels(d + 1, flow, sp.group(p)):
                        scatter_copy(flow, d, p, True)[0].wait_recv()
                        total = total + rcv[d, pl.ds(at, count)].astype(F32)
                    snd[d, pl.ds(at, count)] = total.astype(BF16)
                    going.start()

                when(cond, on)

    def make_gdown(o):
        block = jnp.concatenate([gall[o, sd.size + j] for j in range(sd.size)], axis=1)
        at = pl.multiple_of(sd.second(o) * LANE, LANE)
        gdv[:, pl.ds(at, sd.size * LANE)] = mm(hidt[...], block).astype(BF16)

    done = 0
    for d in range(hops, 0, -1):
        scatter_step(d)
        while done < n * (hops - d + 1) // hops:
            make_gdown(done)
            done += 1
    for g in range(GROUPS if direct else 0):
        at = (ringed + g * per) * LANE
        block = jnp.concatenate([gdir[g, per + j] for j in range(per)], axis=1)
        gdv[:, at:at + per * LANE] = mm(hidt[...], block).astype(BF16)
    store = pltpu.make_async_copy(gdv, gdown, osem)
    store.start()

    make_part(0, z, 0)
    make_part(0, z, 1)
    for p, (at, count, _) in enumerate(sp.pieces):
        block = pl.ds(at, count)
        cond = None
        for flow in range(2):
            if travels(1, flow, sp.group(p)):
                came, cond = scatter_copy(flow, 0, p, True)
                when(cond, came.wait_recv)

        def on(block=block, p=p):
            total = part[0, block]
            for flow in range(2):
                if travels(1, flow, sp.group(p)):
                    total = total + flows[flow][1][0, block].astype(F32)
            ybuf[block] = total.astype(BF16)

        if cond is not None:
            ybuf[block] = jnp.zeros_like(ybuf[block])
        when(cond, on)

    for j in range(sp.slots):
        snd3[:, j] = ybuf[j].reshape(a_n, rows_a, LANE)
    arrive(exchange("a", snd3, rcv3, s3, r3))
    split_store(snd4, 0, regroup(rcv3, a_n, ny), ny)
    arrive(exchange("y", snd4, rcv4, s4, r4))

    back = [rcv4[:, j].reshape(slots, LANE) for j in range(sp.slots)]
    back_in, back_out = jnp.concatenate(back[:size], axis=1), jnp.concatenate(back[size:], axis=1)
    eye = jnp.where(iota((tok_n, tok_n), 0) == iota((tok_n, tok_n), 1), 1.0, 0.0).astype(BF16)
    high = gate_of.astype(BF16)
    low = (gate_of - high.astype(F32)).astype(BF16)
    high_t, low_t, pick_t = [mm(eye, v, 1, 1).astype(BF16) for v in (high, low, pick)]
    mixed_part = (mm(high_t, back_out) + mm(low_t, back_out)).astype(BF16)
    gtok_part = mm(pick_t, back_in).astype(BF16)
    shift = 1 if sp.extra else 0

    def place(slot):
        if slot < size:
            return 0 if slot >= sp.base else slot + shift
        return slot - size + sp.base + shift

    for j in range(size):
        fin[z, place(j)] = gtok_part[:, j * LANE:(j + 1) * LANE]
        fin[z, place(size + j)] = mixed_part[:, j * LANE:(j + 1) * LANE]
    inner = mm(back_out, own_columns(sp, cot, sp.second(z), sp.more_second), 1, 1) * pick_f
    inner = jnp.concatenate(
        [jnp.sum(jnp.where(hits[k], inner, 0.0), axis=0, keepdims=True) for k in range(top)], axis=0
    )
    lane, line = iota((tok_n, LANE), 1), iota((tok_n, LANE), 0)
    spread = jnp.where((lane % tok_n == line) & (lane < top * tok_n), 1.0, 0.0)
    mine = iota((top, LANE), 1) // tok_n == iota((top, LANE), 0)

    def exact(a, b, cb):
        return lax.dot_general(
            a, b, (((1,), (cb,)), ((), ())), precision=lax.Precision.HIGHEST, preferred_element_type=F32
        )

    gfin[z] = jnp.sum(jnp.where(mine, exact(inner, spread, 0), 0.0), axis=0, keepdims=True)

    kinds = ((False, False), (True, False), (False, True), (True, True))

    def ranges(o):
        if not sp.extra:
            return [(0, sp.slots, None)]
        out = []
        for first, second in kinds:
            a, b = sp.more_first(o), sp.more_second(o)
            cond = (a if first else jnp.logical_not(a)) & (b if second else jnp.logical_not(b))
            at = 0 if first else 1
            out.append((at, 2 * sp.base + 1 - at + (1 if second else 0), cond))
        return out

    def final_copies(i, o, device):
        out = [(copy(fin.at[o, pl.ds(at, count)], fin.at[o, pl.ds(at, count)], fs.at[i, 0], fr.at[i, 0], device), cond)
               for at, count, cond in ranges(o)]
        out.append((copy(gfin.at[o], gfin.at[o], fs.at[i, 1], fr.at[i, 1], device), None))
        return out

    finals = [final_copies(i, z, (lax.rem(z + i, n), e)) for i in range(1, n)]
    for i in sorted(range(1, n), key=lambda i: -min(i, n - i)):
        for c, cond in finals[i - 1]:
            when(cond, c.start)
    for i in range(1, n):
        for c, cond in final_copies(i, lax.rem(z + n - i, n), (right, e)):
            when(cond, c.wait_recv)

    total = jnp.zeros(gfin.shape[1:], F32)
    for o in range(n):
        total = total + gfin[o]
        for slot, which, tile in sp.static(o):
            (gtok, mixed)[which][:, tile * LANE:(tile + 1) * LANE] = fin[o, place(slot)]
    ggates[...] = exact(jnp.where(mine, total, 0.0), spread, 1)

    for c in sends:
        c.wait_send()
    for way in range(2):

        def left_at(d, carry, way=way):
            for split, pieces_copy, first in ((sd, gather_copy, 0), (sp, scatter_copy, 1)):
                for p in range(len(split.pieces)):
                    if travels(d + 1, way, split.group(p)):
                        c, cond = pieces_copy(way, d + first, p)
                        when(cond, c.wait_send)
            return carry

        for d in range(hops):
            left_at(d, 0)
    for copies in finals:
        for c, cond in copies:
            when(cond, c.wait_send)
    store.wait()


def local(n, n_expert, tokens, route, gate_code, cotangent, w_gate, w_up, w_down):
    tok_n, width = tokens.shape
    top = route.shape[1]
    f = w_gate.shape[2]
    ny, a_n = ROWS_Y, n_expert // ROWS_Y
    slots = n_expert * CAP
    tiles = width // LANE
    direct = DIRECT if tiles > DIRECT else 0
    sd, sp = Split(n, tiles - direct), Split(n, tiles)
    k, np_ = sp.slots, len(sp.pieces)
    kd, npd = sd.slots, len(sd.pieces)
    groups, per2 = (GROUPS, 2 * direct // GROUPS) if direct else (1, 1)
    hops = n // 2
    vmem = pl.BlockSpec(memory_space=pltpu.VMEM)
    anyw = pl.BlockSpec(memory_space=pl.ANY)
    dma = pltpu.SemaphoreType.DMA

    def b16(*shape):
        return pltpu.VMEM(shape, BF16)

    def f32(*shape):
        return pltpu.VMEM(shape, F32)

    rows_y, rows_a = a_n * CAP, ny * CAP
    mixed, gtok, ggates, gdown = pl.pallas_call(
        functools.partial(kernel, n, n_expert),
        out_shape=(
            jax.ShapeDtypeStruct((tok_n, width), BF16),
            jax.ShapeDtypeStruct((tok_n, width), BF16),
            jax.ShapeDtypeStruct((top, tok_n), F32),
            jax.ShapeDtypeStruct((f, width), BF16),
        ),
        in_specs=[anyw] * 7,
        out_specs=(vmem, vmem, vmem, anyw),
        scratch_shapes=[
            pltpu.VMEM((top, tok_n), jnp.int32), pltpu.VMEM((top, tok_n), jnp.int32),
            b16(tok_n, width), b16(tok_n, width),
            b16(width + LANE, 2 * f), b16(f, width), b16(f, width),
            b16(ny, kd, rows_y, LANE), b16(ny, kd, rows_y, LANE), b16(a_n, kd, rows_a, LANE),
            b16(n, kd, slots, LANE),
            b16(groups, ny, per2, rows_y, LANE), b16(groups, ny, per2, rows_y, LANE),
            b16(groups, a_n, per2, rows_a, LANE), b16(groups, per2, slots, LANE),
            f32(slots, 2 * f), f32(slots, f), f32(2, k, slots, LANE),
            b16(slots, f), b16(f, slots), b16(slots, 2 * f),
            b16(hops + 1, k, slots, LANE), b16(hops, k, slots, LANE),
            b16(hops + 1, k, slots, LANE), b16(hops, k, slots, LANE),
            b16(k, slots, LANE), b16(a_n, k, rows_a, LANE), b16(a_n, k, rows_a, LANE),
            b16(ny, k, rows_y, LANE), b16(ny, k, rows_y, LANE),
            b16(n, k, tok_n, LANE), f32(n, 1, LANE),
            dma((4,)), dma((3,)), dma((ny,)), dma((ny,)), dma((a_n,)), dma((a_n,)),
            dma((groups, ny)), dma((groups, ny)), dma((groups, a_n)), dma((groups, a_n)),
            dma((2, hops, npd)), dma((2, hops + 1, npd)),
            dma((hops + 1, np_)), dma((hops, np_)), dma((hops + 1, np_)), dma((hops, np_)),
            dma((a_n,)), dma((a_n,)), dma((ny,)), dma((ny,)),
            dma((n, 2)), dma((n, 2)), dma,
        ],
        compiler_params=pltpu.CompilerParams(
            collective_id=0, has_side_effects=True, vmem_limit_bytes=60 * 1024 * 1024
        ),
        name="moe_step",
    )(route.T, gate_code.T, tokens, cotangent, w_gate[0], w_up[0], w_down[0])
    return mixed, gtok, ggates.T, gdown[None]


def solution(mesh):
    n, n_expert = mesh.shape["dp"], mesh.shape["expert"]
    return jax.shard_map(
        functools.partial(local, n, n_expert),
        mesh=mesh,
        in_specs=(
            P("expert", None),
            P("expert", None),
            P("expert", None),
            P("expert", None),
            P("expert", None, "dp"),
            P("expert", None, "dp"),
            P("expert", "dp", None),
        ),
        out_specs=(
            P("expert", None),
            P("expert", None),
            P("expert", None),
            P("expert", "dp", None),
        ),
        check_vma=False,
    )
```

```python
import functools

import jax
import jax.numpy as jnp
from jax import lax
from jax.experimental import pallas as pl
from jax.experimental.pallas import tpu as pltpu
from jax.sharding import PartitionSpec as P

ROWS_Y = 8
CORES = 2
CAP = 2
LANE = 128
F32 = jnp.float32
BF16 = jnp.bfloat16
MESH = pl.DeviceIdType.MESH
DIRECT = (4, 4)
TURN = 1


def mm(a, b, ca=1, cb=0):
    return lax.dot_general(a, b, (((ca,), (cb,)), ((), ())), preferred_element_type=F32)


def when(cond, body):
    if cond is None:
        body()
    else:
        pl.when(cond)(body)


class Split:
    def __init__(self, n, tiles):
        self.n, self.tiles = n, tiles
        self.base, self.extra = tiles // n, tiles % n
        self.size = self.base + (1 if self.extra else 0)
        self.slots = 2 * self.size
        self.pieces = [(j, 1, None) for j in range(self.base)]
        if self.extra:
            self.pieces.append((self.base, 1, self.more_first))
        self.half = len(self.pieces)
        self.pieces += [(self.size + j, 1, None) for j in range(self.base)]
        if self.extra:
            self.pieces.append((self.size + self.base, 1, self.more_second))

    def more_first(self, o):
        return o < self.extra

    def more_second(self, o):
        return o >= self.n - self.extra

    def first(self, o):
        return self.base * o + jnp.minimum(o, self.extra)

    def second(self, o):
        return self.base * o + jnp.maximum(o - (self.n - self.extra), 0)

    def group(self, p):
        return 0 if p < self.half else 1

    def static(self, o):
        a = self.base * o + min(o, self.extra)
        b = self.base * o + max(o - (self.n - self.extra), 0)
        na = self.base + (1 if o < self.extra else 0)
        nb = self.base + (1 if o >= self.n - self.extra and self.extra else 0)
        return [(j, 0, a + j) for j in range(na)] + [(self.size + j, 1, b + j) for j in range(nb)]


def iota(shape, axis):
    return lax.broadcasted_iota(jnp.int32, shape, axis)


def kernel(
    n, n_expert,
    route_h, codes_h, tokens_h, cot_h, wg, wu, wd,
    mixed, gtok, ggates, gdown,
    route, codes, tokens, cot, wgu, wdv, gdv, snd1, rcv1, snd2, gall, snd1d, rcv1d, snd2d, gdir, pre, ghid, part, hid, hidt, ggu,
    sndl, rcvl, sndr, rcvr, ybuf, snd3, rcv3, snd4, rcv4, snd5, rcv5, snd6, rcv6, zsnd, zrcv, fin, gfin,
    isem, wsem, s1, r1, s2, r2, s1d, r1d, s2d, r2d, gs, gr, ls, lr, rs, rr, s3, r3, s4, r4, fs, fr, osem, s5, r5, s6, r6, zs, zr,
):
    ny = ROWS_Y
    a_n = n_expert // ny
    rows_y, rows_a = a_n * CAP, ny * CAP
    slots = n_expert * CAP
    top, tok_n = route.shape
    width = tokens.shape[1]
    tiles = width // LANE
    direct = DIRECT if tiles > sum(DIRECT) else ()
    ringed = tiles - sum(direct)
    m = n // 2 if n % 2 == 0 else n
    sd, sp = Split(m, ringed), Split(n, tiles)
    late = sp.extra
    kept = tiles - late
    per_b = late // 2
    sb = Split(n, kept)
    size, chunk_w = sb.size, sb.size * LANE
    hops, hops_in = n // 2, m // 2

    def travels(hop, way, group):
        return hop < hops or (hop == hops and (n % 2 == 1 or way == group))

    def travels_in(hop, way, group):
        return hop < hops_in or (hop == hops_in and (m % 2 == 1 or way == group))

    z = lax.axis_index("dp")
    e = lax.axis_index("expert")
    core = lax.rem(e, CORES)
    y = lax.rem(e // CORES, ny)
    x = e // (CORES * ny)
    xc = x * CORES + core
    right, left = lax.rem(z + 1, n), lax.rem(z + n - 1, n)
    zm = lax.rem(z, m)

    def y_peer(i):
        yp = lax.rem(y + i, ny)
        return yp, (z, (x * ny + yp) * CORES + core)

    def a_peer(i):
        ap = lax.rem(xc + i, a_n)
        return ap, (z, ((ap // CORES) * ny + y) * CORES + lax.rem(ap, CORES))

    def copy(src, dst, ssem, rsem, device):
        return pltpu.make_async_remote_copy(
            src_ref=src, dst_ref=dst, send_sem=ssem, recv_sem=rsem, device_id=device, device_id_type=MESH
        )

    for o in range(m):
        held = {slot for slot, _, _ in sd.static(o)}
        for j in range(sd.slots):
            if j not in held:
                gall[o, j] = jnp.zeros((slots, LANE), BF16)
    if sp.extra or sd.extra:
        wgu[pl.ds(width, LANE), :] = jnp.zeros((LANE, wgu.shape[1]), BF16)

    barrier = pltpu.get_barrier_semaphore()
    peers = [y_peer(i)[1] for i in range(1, ny)] + [a_peer(i)[1] for i in range(1, a_n)]
    peers += [(lax.rem(z + i, n), e) for i in range(1, n)]
    for peer in peers:
        pl.semaphore_signal(barrier, inc=1, device_id=peer, device_id_type=MESH)

    f = wdv.shape[0]
    inputs = [
        pltpu.make_async_copy(src, dst, isem.at[i])
        for i, (src, dst) in enumerate(((route_h, route), (codes_h, codes), (tokens_h, tokens), (cot_h, cot)))
    ]
    loads = [
        pltpu.make_async_copy(wg, wgu.at[pl.ds(0, width), pl.ds(0, f)], wsem.at[0]),
        pltpu.make_async_copy(wu, wgu.at[pl.ds(0, width), pl.ds(f, f)], wsem.at[1]),
        pltpu.make_async_copy(wd, wdv, wsem.at[2]),
    ]
    for load in inputs + loads:
        load.start()
    pre[...] = jnp.zeros_like(pre)
    ghid[...] = jnp.zeros_like(ghid)
    for load in inputs:
        load.wait()

    code_f = codes[...].astype(F32)
    gates = code_f / jnp.sum(code_f, axis=0, keepdims=True)
    earlier = jnp.where(iota((tok_n, tok_n), 0) < iota((tok_n, tok_n), 1), 1.0, 0.0).astype(BF16)

    def slots_of(s_y, s_xc):
        s_expert = ((s_xc // CORES) * ny + s_y) * CORES + s_xc % CORES
        hits = [route[k:k + 1, :] == s_expert for k in range(top)]
        named = jnp.zeros((slots, tok_n), F32)
        gate_of = jnp.zeros((slots, tok_n), F32)
        for k in range(top):
            named = named + jnp.where(hits[k], 1.0, 0.0)
            gate_of = gate_of + jnp.where(hits[k], gates[k:k + 1, :], 0.0)
        before = mm(named.astype(BF16), earlier)
        pick_f = jnp.where(before == (s_id % CAP).astype(F32), named, 0.0)
        gate_of = gate_of * pick_f
        return hits, pick_f, gate_of, jnp.sum(gate_of, axis=1, keepdims=True)

    s_id = iota((slots, tok_n), 0)
    by_y = slots_of(s_id // rows_y, (s_id // CAP) % a_n)
    by_a = slots_of((s_id // CAP) % ny, s_id // rows_a)

    def own_columns(split, ref, which, o):
        start, more = ((split.first, split.more_first), (split.second, split.more_second))[which]
        parts = []
        for j in range(split.size):
            at = jnp.minimum(start(o) + j, tiles - 1)
            block = ref[:, pl.ds(pl.multiple_of(at * LANE, LANE), LANE)]
            if j >= split.base:
                block = jnp.where(more(o), block, jnp.zeros_like(block))
            parts.append(block)
        return jnp.concatenate(parts, axis=1)

    def split_store(ref, slot0, value, groups):
        for j in range(value.shape[1] // LANE):
            ref[:, slot0 + j] = value[:, j * LANE:(j + 1) * LANE].reshape(groups, slots // groups, LANE)

    def pick_first(order, columns):
        return mm(order[1].astype(BF16), columns).astype(BF16)

    def pick_second(order, columns):
        return (mm(order[1].astype(BF16), columns) * order[3]).astype(BF16)

    split_store(snd1, 0, pick_first(by_y, own_columns(sd, tokens, 0, zm)), ny)
    split_store(snd1, sd.size, pick_second(by_y, own_columns(sd, cot, 1, zm)), ny)

    pl.semaphore_wait(barrier, len(peers))

    sends = []
    axes = {"y": (y_peer, ny, y), "a": (a_peer, a_n, xc)}

    def exchange(axis, src, dst, ssem, rsem, by_rows=False):
        peer, count, me = axes[axis]
        height = slots // count
        rows = pl.ds(pl.multiple_of(me * height, height), height)
        to = dst.at[:, rows] if by_rows else dst.at[me]
        copies = []
        for i in range(1, count):
            b, device = peer(i)
            copies.append(copy(src.at[b], to, ssem.at[i], rsem.at[i], device))
        for c in copies:
            c.start()
        if by_rows:
            for j in range(src.shape[1]):
                dst[j, rows] = src[me, j]
        else:
            dst[me] = src[me]
        sends.extend(copies)
        return copies

    def arrive(copies):
        for c in copies:
            c.wait_recv()

    def permute(whole, outer, inner):
        to, at = iota((slots, slots), 0), iota((slots, slots), 1)
        want = ((to // CAP) % outer) * (inner * CAP) + (to // (outer * CAP)) * CAP + to % CAP
        move = jnp.where(at == want, 1.0, 0.0).astype(BF16)
        return mm(move, whole).astype(BF16)

    def regroup(src, outer, inner):
        whole = jnp.concatenate([src[:, j].reshape(slots, LANE) for j in range(src.shape[1])], axis=1)
        return permute(whole, outer, inner)

    def columns_of(g):
        at = (ringed + sum(direct[:g])) * LANE
        return slice(at, at + direct[g] * LANE)

    def tiles_of(ref, g):
        return ref.at[g, :, pl.ds(0, 2 * direct[g])]

    def build(g, order, groups):
        split_store(tiles_of(snd1d, g), 0, pick_first(order, tokens[:, columns_of(g)]), groups)
        split_store(tiles_of(snd1d, g), direct[g], pick_second(order, cot[:, columns_of(g)]), groups)

    def direct_out(g, axis):
        return exchange(axis, tiles_of(snd1d, g), tiles_of(rcv1d, g), s1d.at[g], r1d.at[g])

    def direct_on(g, axis, outer, inner):
        split_store(snd2d.at[g], 0, regroup(tiles_of(rcv1d, g), outer, inner), inner)
        to = gdir.at[g, pl.ds(0, 2 * direct[g])]
        return exchange(axis, tiles_of(snd2d, g), to, s2d.at[g], r2d.at[g], True)

    own = exchange("y", snd1, rcv1, s1, r1)
    if direct:
        build(1, by_a, a_n)
        second = direct_out(1, "a")
    arrive(own)
    split_store(snd2, 0, regroup(rcv1, ny, a_n), a_n)
    own = exchange("a", snd2, gall.at[zm], s2, r2, True)
    if direct:
        build(0, by_y, ny)
        first = direct_out(0, "y")
        arrive(second)
        second = direct_on(1, "y", a_n, ny)
    arrive(own)

    def first_turn():
        arrive(first)
        return direct_on(0, "a", ny, a_n)

    def direct_use(g):
        block = jnp.concatenate([gdir[g, j] for j in range(direct[g])], axis=1)
        pre[...] += mm(block, wgu[columns_of(g), :])
        block = jnp.concatenate([gdir[g, direct[g] + j] for j in range(direct[g])], axis=1)
        ghid[...] += mm(block, wdv[:, columns_of(g)], 1, 1)

    def to_right(d):
        return lax.rem(z + n - d, n), (right, e)

    def to_left(d):
        return lax.rem(z + d, n), (left, e)

    ways = (to_right, to_left)

    def gather_copy(way, d, p, arrival=False):
        o, device = ways[way](d)
        o = lax.rem(o, m)
        at, count, cond = sd.pieces[p]
        block = gall.at[o, pl.ds(at, count)]
        to = d if arrival else d + 1
        return copy(block, block, gs.at[way, d, p], gr.at[way, to, p], device), cond and cond(o)

    def use_first(o):
        block = jnp.concatenate([gall[o, j] for j in range(sd.size)], axis=1)
        at = pl.multiple_of(sd.first(o) * LANE, LANE)
        pre[...] += mm(block, wgu[pl.ds(at, sd.size * LANE), :])

    def use_second(o):
        block = jnp.concatenate([gall[o, sd.size + j] for j in range(sd.size)], axis=1)
        at = pl.multiple_of(sd.second(o) * LANE, LANE)
        ghid[...] += mm(block, wdv[:, pl.ds(at, sd.size * LANE)], 1, 1)

    def gather_step(d):
        for group, use in ((0, use_first), (1, use_second)):
            for p in range(len(sd.pieces)):
                if sd.group(p) != group:
                    continue
                for way in range(2):
                    if not travels_in(d, way, group):
                        continue
                    came, cond = gather_copy(way, d, p, True)

                    def on(came=came, way=way, p=p, group=group):
                        came.wait_recv()
                        if travels_in(d + 1, way, group):
                            gather_copy(way, d, p)[0].start()

                    when(cond, on)
            for way in range(2):
                if travels_in(d, way, group):
                    use(lax.rem(ways[way](d)[0], m))

    for p in range(len(sd.pieces)):
        for way in range(2):
            if travels_in(1, way, sd.group(p)):
                c, cond = gather_copy(way, 0, p)
                when(cond, c.start)
    for load in loads:
        load.wait()
    use_first(zm)
    use_second(zm)
    for d in range(1, hops_in + 1):
        gather_step(d)
        if direct and d == TURN:
            first = first_turn()
    if direct:
        arrive(second)
        whole = jnp.concatenate([gdir[1, j] for j in range(2 * direct[1])], axis=1)
        whole = permute(whole, ny, a_n)
        for j in range(2 * direct[1]):
            gdir[1, j] = whole[:, j * LANE:(j + 1) * LANE]
        direct_use(1)
        arrive(first)
        direct_use(0)

    gate_pre, up_pre, grad_hidden = pre[:, :f], pre[:, f:], ghid[...]
    sigma = 1.0 / (1.0 + jnp.exp(-gate_pre))
    silu = gate_pre * sigma
    hidden = silu * up_pre
    hid[...] = hidden.astype(BF16)
    hidt[...] = hidden.T.astype(BF16)
    ggu[:, :f] = (grad_hidden * up_pre * sigma * (1.0 + gate_pre * (1.0 - sigma))).astype(BF16)
    ggu[:, f:] = (grad_hidden * silu).astype(BF16)

    def make_part(which, o, group):
        if group == 0:
            at = pl.multiple_of(sb.first(o) * LANE, LANE)
            value = mm(ggu[...], wgu[pl.ds(at, chunk_w), :], 1, 1)
        else:
            at = pl.multiple_of(sb.second(o) * LANE, LANE)
            value = mm(hid[...], wdv[:, pl.ds(at, chunk_w)])
        for j in range(size):
            part[which, group * size + j] = value[:, j * LANE:(j + 1) * LANE]

    flows = ((sndl, rcvl, ls, lr, to_right, (left, e)), (sndr, rcvr, rs, rr, to_left, (right, e)))

    def scatter_copy(flow, d, p, arrival=False):
        snd, rcv, ssem, rsem, owner, device = flows[flow]
        at, count, cond = sb.pieces[p]
        to = d if arrival else d - 1
        c = copy(snd.at[d, pl.ds(at, count)], rcv.at[to, pl.ds(at, count)], ssem.at[d, p], rsem.at[to, p], device)
        return c, cond and cond(owner(d)[0])

    def scatter_step(d):
        for flow in range(2):
            for group in range(2):
                if travels(d, flow, group):
                    make_part(flow, flows[flow][4](d)[0], group)
        for p, (at, count, _) in enumerate(sb.pieces):
            for flow in range(2):
                if not travels(d, flow, sb.group(p)):
                    continue
                snd, rcv = flows[flow][:2]
                going, cond = scatter_copy(flow, d, p)

                def on(flow=flow, snd=snd, rcv=rcv, going=going, p=p, at=at, count=count):
                    total = part[flow, pl.ds(at, count)]
                    if travels(d + 1, flow, sb.group(p)):
                        scatter_copy(flow, d, p, True)[0].wait_recv()
                        total = total + rcv[d, pl.ds(at, count)].astype(F32)
                    snd[d, pl.ds(at, count)] = total.astype(BF16)
                    going.start()

                when(cond, on)

    def make_gdown(o):
        block = jnp.concatenate([gall[o, sd.size + j] for j in range(sd.size)], axis=1)
        at = pl.multiple_of(sd.second(o) * LANE, LANE)
        gdv[:, pl.ds(at, sd.size * LANE)] = mm(hidt[...], block).astype(BF16)

    back_first = []

    def back_start():
        for g in range(2):
            cols = pl.ds((kept + g * per_b) * LANE, per_b * LANE)
            whole = jnp.concatenate([mm(ggu[...], wgu[cols, :], 1, 1), mm(hid[...], wdv[:, cols])], axis=1).astype(BF16)
            if g == 1:
                whole = permute(whole, a_n, ny)
            split_store(snd5.at[g], 0, whole, (a_n, ny)[g])
            back_first.append(exchange("ay"[g], snd5.at[g], rcv5.at[g], s5.at[g], r5.at[g]))

    def back_turn(g):
        arrive(back_first[g])
        outer, inner = ((a_n, ny), (ny, a_n))[g]
        split_store(snd6.at[g], 0, regroup(rcv5.at[g], outer, inner), inner)
        return exchange("ya"[g], snd6.at[g], rcv6.at[g], s6.at[g], r6.at[g])

    done = 0
    for d in range(hops, 0, -1):
        scatter_step(d)
        if late and d == hops:
            back_start()
        if late and d == max(1, hops - 2):
            back = [back_turn(0)]
        if late and d == max(1, hops - 4):
            back.append(back_turn(1))
        while done < m * (hops - d + 1) // hops:
            make_gdown(done)
            done += 1
    for g in range(len(direct)):
        block = jnp.concatenate([gdir[g, direct[g] + j] for j in range(direct[g])], axis=1)
        gdv[:, columns_of(g)] = mm(hidt[...], block).astype(BF16)
    store = pltpu.make_async_copy(gdv, gdown, osem)
    store.start()

    make_part(0, z, 0)
    make_part(0, z, 1)
    for p, (at, count, _) in enumerate(sb.pieces):
        block = pl.ds(at, count)
        cond = None
        for flow in range(2):
            if travels(1, flow, sb.group(p)):
                came, cond = scatter_copy(flow, 0, p, True)
                when(cond, came.wait_recv)

        def on(block=block, p=p):
            total = part[0, block]
            for flow in range(2):
                if travels(1, flow, sb.group(p)):
                    total = total + flows[flow][1][0, block].astype(F32)
            ybuf[block] = total.astype(BF16)

        if cond is not None:
            ybuf[block] = jnp.zeros_like(ybuf[block])
        when(cond, on)

    def at_home(order, back_in, back_out, cot_columns):
        hits, pick_f, gate_of = order[:3]
        high = gate_of.astype(BF16)
        low = (gate_of - high.astype(F32)).astype(BF16)
        eye = jnp.where(iota((tok_n, tok_n), 0) == iota((tok_n, tok_n), 1), 1.0, 0.0).astype(BF16)
        high_t, low_t, pick_t = [mm(eye, v, 1, 1).astype(BF16) for v in (high, low, pick_f.astype(BF16))]
        mixed_part = (mm(high_t, back_out) + mm(low_t, back_out)).astype(BF16)
        gtok_part = mm(pick_t, back_in).astype(BF16)
        inner = mm(back_out, cot_columns, 1, 1) * pick_f
        inner = jnp.concatenate(
            [jnp.sum(jnp.where(hits[k], inner, 0.0), axis=0, keepdims=True) for k in range(top)], axis=0
        )
        return gtok_part, mixed_part, inner

    def halves(ref, half):
        blocks = [ref[:, j].reshape(slots, LANE) for j in range(2 * half)]
        return jnp.concatenate(blocks[:half], axis=1), jnp.concatenate(blocks[half:], axis=1)

    for j in range(sb.slots):
        snd3[:, j] = ybuf[j].reshape(a_n, rows_a, LANE)
    own = exchange("a", snd3, rcv3, s3, r3)
    inners = []
    if late:
        for g in range(2):
            arrive(back[g])
            at = (kept + g * per_b) * LANE
            order = (by_y, by_a)[g]
            gtok_part, mixed_part, inner = at_home(order, *halves(rcv6.at[g], per_b), cot[:, at:at + per_b * LANE])
            inners.append(inner)
            for j in range(per_b):
                tile = g * per_b + j
                zsnd[tile, 0] = gtok_part[:, j * LANE:(j + 1) * LANE]
                zsnd[n - late + tile, 1] = mixed_part[:, j * LANE:(j + 1) * LANE]
        for o in range(n):
            if o >= late:
                zsnd[o, 0] = jnp.zeros((tok_n, LANE), BF16)
            if o < n - late:
                zsnd[o, 1] = jnp.zeros((tok_n, LANE), BF16)
        over = []
        for i in range(1, n):
            o = lax.rem(z + i, n)
            over.append(copy(zsnd.at[o], zrcv.at[z], zs.at[i], zr.at[i], (o, e)))
        for c in over:
            c.start()
        zrcv[z] = zsnd[z]
        sends.extend(over)
    arrive(own)
    split_store(snd4, 0, regroup(rcv3, a_n, ny), ny)
    own = exchange("y", snd4, rcv4, s4, r4)
    if late:
        arrive(over)
        sums = [jnp.zeros((tok_n, LANE), F32)] * 2
        for o in range(n):
            for q in range(2):
                sums[q] = sums[q] + zrcv[o, q].astype(F32)
        fin[z, 0] = sums[0].astype(BF16)
        fin[z, 2 * sb.base + 1] = sums[1].astype(BF16)
    arrive(own)

    gtok_part, mixed_part, inner = at_home(
        by_y, *halves(rcv4, size), own_columns(sb, cot, 1, z)
    )
    for more in inners:
        inner = inner + more
    shift = 1 if late else 0
    for j in range(size):
        fin[z, shift + j] = gtok_part[:, j * LANE:(j + 1) * LANE]
        fin[z, shift + size + j] = mixed_part[:, j * LANE:(j + 1) * LANE]
    lane, line = iota((tok_n, LANE), 1), iota((tok_n, LANE), 0)
    spread = jnp.where((lane % tok_n == line) & (lane < top * tok_n), 1.0, 0.0)
    mine = iota((top, LANE), 1) // tok_n == iota((top, LANE), 0)

    def exact(a, b, cb):
        return lax.dot_general(
            a, b, (((1,), (cb,)), ((), ())), precision=lax.Precision.HIGHEST, preferred_element_type=F32
        )

    gfin[z] = jnp.sum(jnp.where(mine, exact(inner, spread, 0), 0.0), axis=0, keepdims=True)

    kinds = ((False, False), (True, False), (False, True), (True, True))

    def ranges(o):
        if not sp.extra:
            return [(0, sp.slots, None)]
        out = []
        for first, second in kinds:
            a, b = sp.more_first(o), sp.more_second(o)
            cond = (a if first else jnp.logical_not(a)) & (b if second else jnp.logical_not(b))
            at = 0 if first else 1
            out.append((at, 2 * sp.base + 1 - at + (1 if second else 0), cond))
        return out

    def final_copies(i, o, device):
        out = [(copy(fin.at[o, pl.ds(at, count)], fin.at[o, pl.ds(at, count)], fs.at[i, 0], fr.at[i, 0], device), cond)
               for at, count, cond in ranges(o)]
        out.append((copy(gfin.at[o], gfin.at[o], fs.at[i, 1], fr.at[i, 1], device), None))
        return out

    finals = [final_copies(i, z, (lax.rem(z + i, n), e)) for i in range(1, n)]
    for i in sorted(range(1, n), key=lambda i: -min(i, n - i)):
        for c, cond in finals[i - 1]:
            when(cond, c.start)
    for i in range(1, n):
        for c, cond in final_copies(i, lax.rem(z + n - i, n), (right, e)):
            when(cond, c.wait_recv)

    total = jnp.zeros(gfin.shape[1:], F32)
    for o in range(n):
        total = total + gfin[o]
        held = [(shift + slot, which, tile) for slot, which, tile in sb.static(o)]
        if late and o < late:
            held.append((0, 0, kept + o))
        if late and o >= n - late:
            held.append((2 * sb.base + 1, 1, kept + o - (n - late)))
        for slot, which, tile in held:
            (gtok, mixed)[which][:, tile * LANE:(tile + 1) * LANE] = fin[o, slot]
    ggates[...] = exact(jnp.where(mine, total, 0.0), spread, 1)

    for c in sends:
        c.wait_send()
    for way in range(2):

        def left_at(d, carry, way=way):
            for split, pieces_copy, first, does in ((sd, gather_copy, 0, travels_in), (sb, scatter_copy, 1, travels)):
                for p in range(len(split.pieces)):
                    if does(d + 1, way, split.group(p)):
                        c, cond = pieces_copy(way, d + first, p)
                        when(cond, c.wait_send)
            return carry

        for d in range(hops):
            left_at(d, 0)
    for copies in finals:
        for c, cond in copies:
            when(cond, c.wait_send)
    store.wait()


def hand_over(*refs):
    sem = refs[8]
    copies = [pltpu.make_async_copy(refs[i], refs[4 + i], sem.at[i]) for i in range(4)]
    for c in copies:
        c.start()
    for c in copies:
        c.wait()


def local(n, n_expert, tokens, route, gate_code, cotangent, w_gate, w_up, w_down):
    tok_n, width = tokens.shape
    top = route.shape[1]
    f = w_gate.shape[2]
    ny, a_n = ROWS_Y, n_expert // ROWS_Y
    slots = n_expert * CAP
    tiles = width // LANE
    direct = DIRECT if tiles > sum(DIRECT) else ()
    m = n // 2 if n % 2 == 0 else n
    sd, sp = Split(m, tiles - sum(direct)), Split(n, tiles)
    late = sp.extra
    sb = Split(n, tiles - late)
    k, np_ = sb.slots, len(sb.pieces)
    kb = max(1, late)
    kd, npd = sd.slots, len(sd.pieces)
    groups, per2 = (2, 2 * max(direct)) if direct else (1, 1)
    hops, hops_in = n // 2, m // 2
    vmem = pl.BlockSpec(memory_space=pltpu.VMEM)
    anyw = pl.BlockSpec(memory_space=pl.ANY)
    dma = pltpu.SemaphoreType.DMA

    def b16(*shape):
        return pltpu.VMEM(shape, BF16)

    def f32(*shape):
        return pltpu.VMEM(shape, F32)

    rows_y, rows_a = a_n * CAP, ny * CAP
    results = pl.pallas_call(
        functools.partial(kernel, n, n_expert),
        out_shape=(
            jax.ShapeDtypeStruct((tok_n, width), BF16),
            jax.ShapeDtypeStruct((tok_n, width), BF16),
            jax.ShapeDtypeStruct((top, tok_n), F32),
            jax.ShapeDtypeStruct((f, width), BF16),
        ),
        in_specs=[anyw] * 7,
        out_specs=(vmem, vmem, vmem, anyw),
        scratch_shapes=[
            pltpu.VMEM((top, tok_n), jnp.int32), pltpu.VMEM((top, tok_n), jnp.int32),
            b16(tok_n, width), b16(tok_n, width),
            b16(width + LANE, 2 * f), b16(f, width), b16(f, width),
            b16(ny, kd, rows_y, LANE), b16(ny, kd, rows_y, LANE), b16(a_n, kd, rows_a, LANE),
            b16(m, kd, slots, LANE),
            b16(groups, ny, per2, rows_y, LANE), b16(groups, ny, per2, rows_y, LANE),
            b16(groups, a_n, per2, rows_a, LANE), b16(groups, per2, slots, LANE),
            f32(slots, 2 * f), f32(slots, f), f32(2, k, slots, LANE),
            b16(slots, f), b16(f, slots), b16(slots, 2 * f),
            b16(hops + 1, k, slots, LANE), b16(hops, k, slots, LANE),
            b16(hops + 1, k, slots, LANE), b16(hops, k, slots, LANE),
            b16(k, slots, LANE), b16(a_n, k, rows_a, LANE), b16(a_n, k, rows_a, LANE),
            b16(ny, k, rows_y, LANE), b16(ny, k, rows_y, LANE),
            b16(2, a_n, kb, rows_a, LANE), b16(2, a_n, kb, rows_a, LANE),
            b16(2, ny, kb, rows_y, LANE), b16(2, ny, kb, rows_y, LANE),
            b16(n, 2, tok_n, LANE), b16(n, 2, tok_n, LANE),
            b16(n, sp.slots, tok_n, LANE), f32(n, 1, LANE),
            dma((4,)), dma((3,)), dma((ny,)), dma((ny,)), dma((a_n,)), dma((a_n,)),
            dma((groups, ny)), dma((groups, ny)), dma((groups, a_n)), dma((groups, a_n)),
            dma((2, hops_in, npd)), dma((2, hops_in + 1, npd)),
            dma((hops + 1, np_)), dma((hops, np_)), dma((hops + 1, np_)), dma((hops, np_)),
            dma((a_n,)), dma((a_n,)), dma((ny,)), dma((ny,)),
            dma((n, 2)), dma((n, 2)), dma,
            dma((2, a_n)), dma((2, a_n)), dma((2, ny)), dma((2, ny)), dma((n,)), dma((n,)),
        ],
        compiler_params=pltpu.CompilerParams(
            collective_id=0, has_side_effects=True, vmem_limit_bytes=60 * 1024 * 1024
        ),
        name="moe_step",
    )(route.T, gate_code.T, tokens, cotangent, w_gate[0], w_up[0], w_down[0])
    mixed, gtok, ggates, gdown = pl.pallas_call(
        hand_over,
        out_shape=tuple(jax.ShapeDtypeStruct(v.shape, v.dtype) for v in results),
        in_specs=[vmem] * 4,
        out_specs=(anyw,) * 4,
        scratch_shapes=[dma((4,))],
        name="hand_over",
    )(*results)
    return mixed, gtok, ggates.T, gdown[None]


def solution(mesh):
    n, n_expert = mesh.shape["dp"], mesh.shape["expert"]
    return jax.shard_map(
        functools.partial(local, n, n_expert),
        mesh=mesh,
        in_specs=(
            P("expert", None),
            P("expert", None),
            P("expert", None),
            P("expert", None),
            P("expert", None, "dp"),
            P("expert", None, "dp"),
            P("expert", "dp", None),
        ),
        out_specs=(
            P("expert", None),
            P("expert", None),
            P("expert", None),
            P("expert", "dp", None),
        ),
        check_vma=False,
    )
```

```python
import functools

import jax
import jax.numpy as jnp
from jax import lax
from jax.experimental import pallas as pl
from jax.experimental.pallas import tpu as pltpu
from jax.sharding import PartitionSpec as P

ROWS_Y = 8
CORES = 2
CAP = 2
LANE = 128
F32 = jnp.float32
BF16 = jnp.bfloat16
MESH = pl.DeviceIdType.MESH
DIRECT = (4, 10)
TURN = 1


def mm(a, b, ca=1, cb=0):
    return lax.dot_general(a, b, (((ca,), (cb,)), ((), ())), preferred_element_type=F32)


def when(cond, body):
    if cond is None:
        body()
    else:
        pl.when(cond)(body)


class Split:
    def __init__(self, n, tiles):
        self.n, self.tiles = n, tiles
        self.base, self.extra = tiles // n, tiles % n
        self.size = self.base + (1 if self.extra else 0)
        self.slots = 2 * self.size
        self.pieces = [(j, 1, None) for j in range(self.base)]
        if self.extra:
            self.pieces.append((self.base, 1, self.more_first))
        self.half = len(self.pieces)
        self.pieces += [(self.size + j, 1, None) for j in range(self.base)]
        if self.extra:
            self.pieces.append((self.size + self.base, 1, self.more_second))

    def more_first(self, o):
        return o < self.extra

    def more_second(self, o):
        return o >= self.n - self.extra

    def first(self, o):
        return self.base * o + jnp.minimum(o, self.extra)

    def second(self, o):
        return self.base * o + jnp.maximum(o - (self.n - self.extra), 0)

    def group(self, p):
        return 0 if p < self.half else 1

    def static(self, o):
        a = self.base * o + min(o, self.extra)
        b = self.base * o + max(o - (self.n - self.extra), 0)
        na = self.base + (1 if o < self.extra else 0)
        nb = self.base + (1 if o >= self.n - self.extra and self.extra else 0)
        return [(j, 0, a + j) for j in range(na)] + [(self.size + j, 1, b + j) for j in range(nb)]


def iota(shape, axis):
    return lax.broadcasted_iota(jnp.int32, shape, axis)


def kernel(
    n, n_expert,
    route_h, codes_h, tokens_h, cot_h, wg, wu, wd,
    mixed, gtok, ggates, gdown,
    route, codes, tokens, cot, wgu, wdv, gdv, snd1, rcv1, snd2, gall, snd1d, rcv1d, snd2d, gdir, pre, ghid, part, hid, hidt, ggu,
    sndl, rcvl, sndr, rcvr, ybuf, snd3, rcv3, snd4, rcv4, snd5, rcv5, snd6, rcv6, zsnd, zrcv, fin, gfin,
    isem, wsem, s1, r1, s2, r2, s1d, r1d, s2d, r2d, gs, gr, ls, lr, rs, rr, s3, r3, s4, r4, fs, fr, osem, s5, r5, s6, r6, zs, zr,
):
    ny = ROWS_Y
    a_n = n_expert // ny
    rows_y, rows_a = a_n * CAP, ny * CAP
    slots = n_expert * CAP
    top, tok_n = route.shape
    width = tokens.shape[1]
    tiles = width // LANE
    direct = DIRECT if tiles > sum(DIRECT) else ()
    ringed = tiles - sum(direct)
    m = n // 2 if n % 2 == 0 else n
    sd, sp = Split(m, ringed), Split(n, tiles)
    late = sp.extra
    kept = tiles - late
    per_b = late // 2
    sb = Split(n, kept)
    size, chunk_w = sb.size, sb.size * LANE
    hops, hops_in = n // 2, m // 2

    def travels(hop, way, group):
        return hop < hops or (hop == hops and (n % 2 == 1 or way == group))

    def travels_in(hop, way, group):
        return hop < hops_in or (hop == hops_in and (m % 2 == 1 or way == group))

    z = lax.axis_index("dp")
    e = lax.axis_index("expert")
    core = lax.rem(e, CORES)
    y = lax.rem(e // CORES, ny)
    x = e // (CORES * ny)
    xc = x * CORES + core
    right, left = lax.rem(z + 1, n), lax.rem(z + n - 1, n)
    zm = lax.rem(z, m)

    def y_peer(i):
        yp = lax.rem(y + i, ny)
        return yp, (z, (x * ny + yp) * CORES + core)

    def a_peer(i):
        ap = lax.rem(xc + i, a_n)
        return ap, (z, ((ap // CORES) * ny + y) * CORES + lax.rem(ap, CORES))

    def copy(src, dst, ssem, rsem, device):
        return pltpu.make_async_remote_copy(
            src_ref=src, dst_ref=dst, send_sem=ssem, recv_sem=rsem, device_id=device, device_id_type=MESH
        )

    for o in range(m):
        held = {slot for slot, _, _ in sd.static(o)}
        for j in range(sd.slots):
            if j not in held:
                gall[o, j] = jnp.zeros((slots, LANE), BF16)
    if sp.extra or sd.extra:
        wgu[pl.ds(width, LANE), :] = jnp.zeros((LANE, wgu.shape[1]), BF16)

    barrier = pltpu.get_barrier_semaphore()
    peers = [y_peer(i)[1] for i in range(1, ny)] + [a_peer(i)[1] for i in range(1, a_n)]
    peers += [(lax.rem(z + i, n), e) for i in range(1, n)]
    for peer in peers:
        pl.semaphore_signal(barrier, inc=1, device_id=peer, device_id_type=MESH)

    f = wdv.shape[0]
    inputs = [
        pltpu.make_async_copy(src, dst, isem.at[i])
        for i, (src, dst) in enumerate(((route_h, route), (codes_h, codes), (tokens_h, tokens), (cot_h, cot)))
    ]
    loads = [
        pltpu.make_async_copy(wg, wgu.at[pl.ds(0, width), pl.ds(0, f)], wsem.at[0]),
        pltpu.make_async_copy(wu, wgu.at[pl.ds(0, width), pl.ds(f, f)], wsem.at[1]),
        pltpu.make_async_copy(wd, wdv, wsem.at[2]),
    ]
    for load in inputs + loads:
        load.start()
    pre[...] = jnp.zeros_like(pre)
    ghid[...] = jnp.zeros_like(ghid)
    for load in inputs:
        load.wait()

    code_f = codes[...].astype(F32)
    gates = code_f / jnp.sum(code_f, axis=0, keepdims=True)
    earlier = jnp.where(iota((tok_n, tok_n), 0) < iota((tok_n, tok_n), 1), 1.0, 0.0).astype(BF16)

    def slots_of(s_y, s_xc):
        s_expert = ((s_xc // CORES) * ny + s_y) * CORES + s_xc % CORES
        hits = [route[k:k + 1, :] == s_expert for k in range(top)]
        named = jnp.zeros((slots, tok_n), F32)
        gate_of = jnp.zeros((slots, tok_n), F32)
        for k in range(top):
            named = named + jnp.where(hits[k], 1.0, 0.0)
            gate_of = gate_of + jnp.where(hits[k], gates[k:k + 1, :], 0.0)
        before = mm(named.astype(BF16), earlier)
        pick_f = jnp.where(before == (s_id % CAP).astype(F32), named, 0.0)
        gate_of = gate_of * pick_f
        return hits, pick_f, gate_of, jnp.sum(gate_of, axis=1, keepdims=True)

    s_id = iota((slots, tok_n), 0)
    by_y = slots_of(s_id // rows_y, (s_id // CAP) % a_n)
    by_a = slots_of((s_id // CAP) % ny, s_id // rows_a)

    def own_columns(split, ref, which, o):
        start, more = ((split.first, split.more_first), (split.second, split.more_second))[which]
        parts = []
        for j in range(split.size):
            at = jnp.minimum(start(o) + j, tiles - 1)
            block = ref[:, pl.ds(pl.multiple_of(at * LANE, LANE), LANE)]
            if j >= split.base:
                block = jnp.where(more(o), block, jnp.zeros_like(block))
            parts.append(block)
        return jnp.concatenate(parts, axis=1)

    def split_store(ref, slot0, value, groups):
        for j in range(value.shape[1] // LANE):
            ref[:, slot0 + j] = value[:, j * LANE:(j + 1) * LANE].reshape(groups, slots // groups, LANE)

    def pick_first(order, columns):
        return mm(order[1].astype(BF16), columns).astype(BF16)

    def pick_second(order, columns):
        return (mm(order[1].astype(BF16), columns) * order[3]).astype(BF16)

    split_store(snd1, 0, pick_first(by_y, own_columns(sd, tokens, 0, zm)), ny)
    split_store(snd1, sd.size, pick_second(by_y, own_columns(sd, cot, 1, zm)), ny)

    pl.semaphore_wait(barrier, len(peers))

    sends = []
    axes = {"y": (y_peer, ny, y), "a": (a_peer, a_n, xc)}

    def exchange(axis, src, dst, ssem, rsem, by_rows=False):
        peer, count, me = axes[axis]
        height = slots // count
        rows = pl.ds(pl.multiple_of(me * height, height), height)
        to = dst.at[:, rows] if by_rows else dst.at[me]
        copies = []
        for i in sorted(range(1, count), key=lambda i: -min(i, count - i)):
            b, device = peer(i)
            copies.append(copy(src.at[b], to, ssem.at[i], rsem.at[i], device))
        for c in copies:
            c.start()
        if by_rows:
            for j in range(src.shape[1]):
                dst[j, rows] = src[me, j]
        else:
            dst[me] = src[me]
        sends.extend(copies)
        return copies

    def arrive(copies):
        for c in copies:
            c.wait_recv()

    def permute(whole, outer, inner):
        to, at = iota((slots, slots), 0), iota((slots, slots), 1)
        want = ((to // CAP) % outer) * (inner * CAP) + (to // (outer * CAP)) * CAP + to % CAP
        move = jnp.where(at == want, 1.0, 0.0).astype(BF16)
        return mm(move, whole).astype(BF16)

    def regroup(src, outer, inner):
        whole = jnp.concatenate([src[:, j].reshape(slots, LANE) for j in range(src.shape[1])], axis=1)
        return permute(whole, outer, inner)

    def columns_of(g):
        at = (ringed + sum(direct[:g])) * LANE
        return slice(at, at + direct[g] * LANE)

    def tiles_of(ref, g):
        return ref.at[g, :, pl.ds(0, 2 * direct[g])]

    def build(g, order, groups):
        split_store(tiles_of(snd1d, g), 0, pick_first(order, tokens[:, columns_of(g)]), groups)
        split_store(tiles_of(snd1d, g), direct[g], pick_second(order, cot[:, columns_of(g)]), groups)

    def direct_out(g, axis):
        return exchange(axis, tiles_of(snd1d, g), tiles_of(rcv1d, g), s1d.at[g], r1d.at[g])

    def direct_on(g, axis, outer, inner):
        split_store(snd2d.at[g], 0, regroup(tiles_of(rcv1d, g), outer, inner), inner)
        to = gdir.at[g, pl.ds(0, 2 * direct[g])]
        return exchange(axis, tiles_of(snd2d, g), to, s2d.at[g], r2d.at[g], True)

    own = exchange("y", snd1, rcv1, s1, r1)
    if direct:
        build(1, by_a, a_n)
        second = direct_out(1, "a")
    arrive(own)
    split_store(snd2, 0, regroup(rcv1, ny, a_n), a_n)
    own = exchange("a", snd2, gall.at[zm], s2, r2, True)
    if direct:
        build(0, by_y, ny)
        first = direct_out(0, "y")
        arrive(second)
        second = direct_on(1, "y", a_n, ny)
    arrive(own)

    def first_turn():
        arrive(first)
        return direct_on(0, "a", ny, a_n)

    def direct_use(g):
        block = jnp.concatenate([gdir[g, j] for j in range(direct[g])], axis=1)
        pre[...] += mm(block, wgu[columns_of(g), :])
        block = jnp.concatenate([gdir[g, direct[g] + j] for j in range(direct[g])], axis=1)
        ghid[...] += mm(block, wdv[:, columns_of(g)], 1, 1)

    def to_right(d):
        return lax.rem(z + n - d, n), (right, e)

    def to_left(d):
        return lax.rem(z + d, n), (left, e)

    ways = (to_right, to_left)

    def gather_copy(way, d, p, arrival=False):
        o, device = ways[way](d)
        o = lax.rem(o, m)
        at, count, cond = sd.pieces[p]
        block = gall.at[o, pl.ds(at, count)]
        to = d if arrival else d + 1
        return copy(block, block, gs.at[way, min(d, hops_in - 1), p], gr.at[way, to, p], device), cond and cond(o)

    def use_first(o):
        block = jnp.concatenate([gall[o, j] for j in range(sd.size)], axis=1)
        at = pl.multiple_of(sd.first(o) * LANE, LANE)
        pre[...] += mm(block, wgu[pl.ds(at, sd.size * LANE), :])

    def use_second(o):
        block = jnp.concatenate([gall[o, sd.size + j] for j in range(sd.size)], axis=1)
        at = pl.multiple_of(sd.second(o) * LANE, LANE)
        ghid[...] += mm(block, wdv[:, pl.ds(at, sd.size * LANE)], 1, 1)

    def gather_step(d):
        for group, use in ((0, use_first), (1, use_second)):
            for p in range(len(sd.pieces)):
                if sd.group(p) != group:
                    continue
                for way in range(2):
                    if not travels_in(d, way, group):
                        continue
                    came, cond = gather_copy(way, d, p, True)

                    def on(came=came, way=way, p=p, group=group):
                        came.wait_recv()
                        if travels_in(d + 1, way, group):
                            gather_copy(way, d, p)[0].start()

                    when(cond, on)
            for way in range(2):
                if travels_in(d, way, group):
                    use(lax.rem(ways[way](d)[0], m))

    for p in range(len(sd.pieces)):
        for way in range(2):
            if travels_in(1, way, sd.group(p)):
                c, cond = gather_copy(way, 0, p)
                when(cond, c.start)
    for load in loads:
        load.wait()
    use_first(zm)
    use_second(zm)
    for d in range(1, hops_in + 1):
        gather_step(d)
        if direct and d == TURN:
            first = first_turn()
    if direct:
        arrive(second)
        whole = jnp.concatenate([gdir[1, j] for j in range(2 * direct[1])], axis=1)
        whole = permute(whole, ny, a_n)
        for j in range(2 * direct[1]):
            gdir[1, j] = whole[:, j * LANE:(j + 1) * LANE]
        direct_use(1)
        arrive(first)
        direct_use(0)

    gate_pre, up_pre, grad_hidden = pre[:, :f], pre[:, f:], ghid[...]
    sigma = 1.0 / (1.0 + jnp.exp(-gate_pre))
    silu = gate_pre * sigma
    hidden = silu * up_pre
    hid[...] = hidden.astype(BF16)
    ggu[:, :f] = (grad_hidden * up_pre * sigma * (1.0 + gate_pre * (1.0 - sigma))).astype(BF16)
    ggu[:, f:] = (grad_hidden * silu).astype(BF16)

    def make_part(which, o, group):
        if group == 0:
            at = pl.multiple_of(sb.first(o) * LANE, LANE)
            value = mm(ggu[...], wgu[pl.ds(at, chunk_w), :], 1, 1)
        else:
            at = pl.multiple_of(sb.second(o) * LANE, LANE)
            value = mm(hid[...], wdv[:, pl.ds(at, chunk_w)])
        for j in range(size):
            part[which, group * size + j] = value[:, j * LANE:(j + 1) * LANE]

    flows = ((sndl, rcvl, ls, lr, to_right, (left, e)), (sndr, rcvr, rs, rr, to_left, (right, e)))

    def scatter_copy(flow, d, p, arrival=False):
        snd, rcv, ssem, rsem, owner, device = flows[flow]
        at, count, cond = sb.pieces[p]
        to = d if arrival else d - 1
        c = copy(snd.at[d, pl.ds(at, count)], rcv.at[to, pl.ds(at, count)], ssem.at[d, p], rsem.at[to, p], device)
        return c, cond and cond(owner(d)[0])

    def scatter_step(d):
        for flow in range(2):
            for group in range(2):
                if travels(d, flow, group):
                    make_part(flow, flows[flow][4](d)[0], group)
        for p, (at, count, _) in enumerate(sb.pieces):
            for flow in range(2):
                if not travels(d, flow, sb.group(p)):
                    continue
                snd, rcv = flows[flow][:2]
                going, cond = scatter_copy(flow, d, p)

                def on(flow=flow, snd=snd, rcv=rcv, going=going, p=p, at=at, count=count):
                    total = part[flow, pl.ds(at, count)]
                    if travels(d + 1, flow, sb.group(p)):
                        scatter_copy(flow, d, p, True)[0].wait_recv()
                        total = total + rcv[d, pl.ds(at, count)].astype(F32)
                    snd[d, pl.ds(at, count)] = total.astype(BF16)
                    going.start()

                when(cond, on)

    def make_gdown(o):
        block = jnp.concatenate([gall[o, sd.size + j] for j in range(sd.size)], axis=1)
        at = pl.multiple_of(sd.second(o) * LANE, LANE)
        gdv[:, pl.ds(at, sd.size * LANE)] = mm(hidt[...], block).astype(BF16)

    back_first = []

    def back_start():
        for g in range(2):
            cols = pl.ds((kept + g * per_b) * LANE, per_b * LANE)
            whole = jnp.concatenate([mm(ggu[...], wgu[cols, :], 1, 1), mm(hid[...], wdv[:, cols])], axis=1).astype(BF16)
            if g == 1:
                whole = permute(whole, a_n, ny)
            split_store(snd5.at[g], 0, whole, (a_n, ny)[g])
            back_first.append(exchange("ay"[g], snd5.at[g], rcv5.at[g], s5.at[g], r5.at[g]))

    def back_turn(g):
        arrive(back_first[g])
        outer, inner = ((a_n, ny), (ny, a_n))[g]
        split_store(snd6.at[g], 0, regroup(rcv5.at[g], outer, inner), inner)
        return exchange("ya"[g], snd6.at[g], rcv6.at[g], s6.at[g], r6.at[g])

    done = 0
    for d in range(hops, 0, -1):
        scatter_step(d)
        if late and d == hops:
            back_start()
        if d == hops:
            hidt[...] = hidden.T.astype(BF16)
        if late and d == max(1, hops - 2):
            back = [back_turn(0)]
        if late and d == max(1, hops - 4):
            back.append(back_turn(1))
        while done < m * (hops - d + 1) // hops:
            make_gdown(done)
            done += 1
    for g in range(len(direct)):
        block = jnp.concatenate([gdir[g, direct[g] + j] for j in range(direct[g])], axis=1)
        gdv[:, columns_of(g)] = mm(hidt[...], block).astype(BF16)
    store = pltpu.make_async_copy(gdv, gdown, osem)
    store.start()

    make_part(0, z, 0)
    make_part(0, z, 1)
    for p, (at, count, _) in enumerate(sb.pieces):
        block = pl.ds(at, count)
        cond = None
        for flow in range(2):
            if travels(1, flow, sb.group(p)):
                came, cond = scatter_copy(flow, 0, p, True)
                when(cond, came.wait_recv)

        def on(block=block, p=p):
            total = part[0, block]
            for flow in range(2):
                if travels(1, flow, sb.group(p)):
                    total = total + flows[flow][1][0, block].astype(F32)
            ybuf[block] = total.astype(BF16)

        if cond is not None:
            ybuf[block] = jnp.zeros_like(ybuf[block])
        when(cond, on)

    def at_home(order, back_in, back_out, cot_columns):
        hits, pick_f, gate_of = order[:3]
        high = gate_of.astype(BF16)
        low = (gate_of - high.astype(F32)).astype(BF16)
        eye = jnp.where(iota((tok_n, tok_n), 0) == iota((tok_n, tok_n), 1), 1.0, 0.0).astype(BF16)
        high_t, low_t, pick_t = [mm(eye, v, 1, 1).astype(BF16) for v in (high, low, pick_f.astype(BF16))]
        mixed_part = (mm(high_t, back_out) + mm(low_t, back_out)).astype(BF16)
        gtok_part = mm(pick_t, back_in).astype(BF16)
        inner = mm(back_out, cot_columns, 1, 1) * pick_f
        inner = jnp.concatenate(
            [jnp.sum(jnp.where(hits[k], inner, 0.0), axis=0, keepdims=True) for k in range(top)], axis=0
        )
        return gtok_part, mixed_part, inner

    def halves(ref, half):
        blocks = [ref[:, j].reshape(slots, LANE) for j in range(2 * half)]
        return jnp.concatenate(blocks[:half], axis=1), jnp.concatenate(blocks[half:], axis=1)

    for j in range(sb.slots):
        snd3[:, j] = ybuf[j].reshape(a_n, rows_a, LANE)
    own = exchange("a", snd3, rcv3, s3, r3)
    inners = []
    if late:
        for g in range(2):
            arrive(back[g])
            at = (kept + g * per_b) * LANE
            order = (by_y, by_a)[g]
            gtok_part, mixed_part, inner = at_home(order, *halves(rcv6.at[g], per_b), cot[:, at:at + per_b * LANE])
            inners.append(inner)
            for j in range(per_b):
                tile = g * per_b + j
                zsnd[tile, 0] = gtok_part[:, j * LANE:(j + 1) * LANE]
                zsnd[n - late + tile, 1] = mixed_part[:, j * LANE:(j + 1) * LANE]
        for o in range(n):
            if o >= late:
                zsnd[o, 0] = jnp.zeros((tok_n, LANE), BF16)
            if o < n - late:
                zsnd[o, 1] = jnp.zeros((tok_n, LANE), BF16)
        over = []
        for i in range(1, n):
            o = lax.rem(z + i, n)
            over.append(copy(zsnd.at[o], zrcv.at[z], zs.at[i], zr.at[i], (o, e)))
        for c in over:
            c.start()
        zrcv[z] = zsnd[z]
        sends.extend(over)
    arrive(own)
    split_store(snd4, 0, regroup(rcv3, a_n, ny), ny)
    own = exchange("y", snd4, rcv4, s4, r4)
    if late:
        arrive(over)
        sums = [jnp.zeros((tok_n, LANE), F32)] * 2
        for o in range(n):
            for q in range(2):
                sums[q] = sums[q] + zrcv[o, q].astype(F32)
        fin[z, 0] = sums[0].astype(BF16)
        fin[z, 2 * sb.base + 1] = sums[1].astype(BF16)
    arrive(own)

    gtok_part, mixed_part, inner = at_home(
        by_y, *halves(rcv4, size), own_columns(sb, cot, 1, z)
    )
    for more in inners:
        inner = inner + more
    shift = 1 if late else 0
    for j in range(size):
        fin[z, shift + j] = gtok_part[:, j * LANE:(j + 1) * LANE]
        fin[z, shift + size + j] = mixed_part[:, j * LANE:(j + 1) * LANE]
    lane, line = iota((tok_n, LANE), 1), iota((tok_n, LANE), 0)
    spread = jnp.where((lane % tok_n == line) & (lane < top * tok_n), 1.0, 0.0)
    mine = iota((top, LANE), 1) // tok_n == iota((top, LANE), 0)

    def exact(a, b, cb):
        return lax.dot_general(
            a, b, (((1,), (cb,)), ((), ())), precision=lax.Precision.HIGHEST, preferred_element_type=F32
        )

    gfin[z] = jnp.sum(jnp.where(mine, exact(inner, spread, 0), 0.0), axis=0, keepdims=True)

    kinds = ((False, False), (True, False), (False, True), (True, True))

    def ranges(o):
        if not sp.extra:
            return [(0, sp.slots, None)]
        out = []
        for first, second in kinds:
            a, b = sp.more_first(o), sp.more_second(o)
            cond = (a if first else jnp.logical_not(a)) & (b if second else jnp.logical_not(b))
            at = 0 if first else 1
            out.append((at, 2 * sp.base + 1 - at + (1 if second else 0), cond))
        return out

    def final_copies(i, o, device):
        out = [(copy(fin.at[o, pl.ds(at, count)], fin.at[o, pl.ds(at, count)], fs.at[i, 0], fr.at[i, 0], device), cond)
               for at, count, cond in ranges(o)]
        out.append((copy(gfin.at[o], gfin.at[o], fs.at[i, 1], fr.at[i, 1], device), None))
        return out

    finals = [final_copies(i, z, (lax.rem(z + i, n), e)) for i in range(1, n)]
    for i in sorted(range(1, n), key=lambda i: -min(i, n - i)):
        for c, cond in finals[i - 1]:
            when(cond, c.start)
    for i in range(1, n):
        for c, cond in final_copies(i, lax.rem(z + n - i, n), (right, e)):
            when(cond, c.wait_recv)

    total = jnp.zeros(gfin.shape[1:], F32)
    for o in range(n):
        total = total + gfin[o]
        held = [(shift + slot, which, tile) for slot, which, tile in sb.static(o)]
        if late and o < late:
            held.append((0, 0, kept + o))
        if late and o >= n - late:
            held.append((2 * sb.base + 1, 1, kept + o - (n - late)))
        for slot, which, tile in held:
            (gtok, mixed)[which][:, tile * LANE:(tile + 1) * LANE] = fin[o, slot]
    ggates[...] = exact(jnp.where(mine, total, 0.0), spread, 1)

    for c in sends:
        c.wait_send()
    for way in range(2):

        def left_at(d, carry, way=way):
            for split, pieces_copy, first, does in ((sd, gather_copy, 0, travels_in), (sb, scatter_copy, 1, travels)):
                for p in range(len(split.pieces)):
                    if does(d + 1, way, split.group(p)):
                        c, cond = pieces_copy(way, d + first, p)
                        when(cond, c.wait_send)
            return carry

        for d in range(hops):
            left_at(d, 0)
    for copies in finals:
        for c, cond in copies:
            when(cond, c.wait_send)
    store.wait()


def hand_over(*refs):
    sem = refs[8]
    copies = [pltpu.make_async_copy(refs[i], refs[4 + i], sem.at[i]) for i in range(4)]
    for c in copies:
        c.start()
    for c in copies:
        c.wait()


def local(n, n_expert, tokens, route, gate_code, cotangent, w_gate, w_up, w_down):
    tok_n, width = tokens.shape
    top = route.shape[1]
    f = w_gate.shape[2]
    ny, a_n = ROWS_Y, n_expert // ROWS_Y
    slots = n_expert * CAP
    tiles = width // LANE
    direct = DIRECT if tiles > sum(DIRECT) else ()
    m = n // 2 if n % 2 == 0 else n
    sd, sp = Split(m, tiles - sum(direct)), Split(n, tiles)
    late = sp.extra
    sb = Split(n, tiles - late)
    k, np_ = sb.slots, len(sb.pieces)
    kb = max(1, late)
    kd, npd = sd.slots, len(sd.pieces)
    groups, per2 = (2, 2 * max(direct)) if direct else (1, 1)
    hops, hops_in = n // 2, m // 2
    vmem = pl.BlockSpec(memory_space=pltpu.VMEM)
    anyw = pl.BlockSpec(memory_space=pl.ANY)
    dma = pltpu.SemaphoreType.DMA

    def b16(*shape):
        return pltpu.VMEM(shape, BF16)

    def f32(*shape):
        return pltpu.VMEM(shape, F32)

    rows_y, rows_a = a_n * CAP, ny * CAP
    results = pl.pallas_call(
        functools.partial(kernel, n, n_expert),
        out_shape=(
            jax.ShapeDtypeStruct((tok_n, width), BF16),
            jax.ShapeDtypeStruct((tok_n, width), BF16),
            jax.ShapeDtypeStruct((top, tok_n), F32),
            jax.ShapeDtypeStruct((f, width), BF16),
        ),
        in_specs=[anyw] * 7,
        out_specs=(vmem, vmem, vmem, anyw),
        scratch_shapes=[
            pltpu.VMEM((top, tok_n), jnp.int32), pltpu.VMEM((top, tok_n), jnp.int32),
            b16(tok_n, width), b16(tok_n, width),
            b16(width + LANE, 2 * f), b16(f, width), b16(f, width),
            b16(ny, kd, rows_y, LANE), b16(ny, kd, rows_y, LANE), b16(a_n, kd, rows_a, LANE),
            b16(m, kd, slots, LANE),
            b16(groups, ny, per2, rows_y, LANE), b16(groups, ny, per2, rows_y, LANE),
            b16(groups, a_n, per2, rows_a, LANE), b16(groups, per2, slots, LANE),
            f32(slots, 2 * f), f32(slots, f), f32(2, k, slots, LANE),
            b16(slots, f), b16(f, slots), b16(slots, 2 * f),
            b16(hops + 1, k, slots, LANE), b16(hops, k, slots, LANE),
            b16(hops + 1, k, slots, LANE), b16(hops, k, slots, LANE),
            b16(k, slots, LANE), b16(a_n, k, rows_a, LANE), b16(a_n, k, rows_a, LANE),
            b16(ny, k, rows_y, LANE), b16(ny, k, rows_y, LANE),
            b16(2, a_n, kb, rows_a, LANE), b16(2, a_n, kb, rows_a, LANE),
            b16(2, ny, kb, rows_y, LANE), b16(2, ny, kb, rows_y, LANE),
            b16(n, 2, tok_n, LANE), b16(n, 2, tok_n, LANE),
            b16(n, sp.slots, tok_n, LANE), f32(n, 1, LANE),
            dma((4,)), dma((3,)), dma((ny,)), dma((ny,)), dma((a_n,)), dma((a_n,)),
            dma((groups, ny)), dma((groups, ny)), dma((groups, a_n)), dma((groups, a_n)),
            dma((2, hops_in, npd)), dma((2, hops_in + 1, npd)),
            dma((hops + 1, np_)), dma((hops, np_)), dma((hops + 1, np_)), dma((hops, np_)),
            dma((a_n,)), dma((a_n,)), dma((ny,)), dma((ny,)),
            dma((n, 2)), dma((n, 2)), dma,
            dma((2, a_n)), dma((2, a_n)), dma((2, ny)), dma((2, ny)), dma((n,)), dma((n,)),
        ],
        compiler_params=pltpu.CompilerParams(
            collective_id=0, has_side_effects=True, vmem_limit_bytes=60 * 1024 * 1024
        ),
        name="moe_step",
    )(route.T, gate_code.T, tokens, cotangent, w_gate[0], w_up[0], w_down[0])
    mixed, gtok, ggates, gdown = pl.pallas_call(
        hand_over,
        out_shape=tuple(jax.ShapeDtypeStruct(v.shape, v.dtype) for v in results),
        in_specs=[vmem] * 4,
        out_specs=(anyw,) * 4,
        scratch_shapes=[dma((4,))],
        name="hand_over",
    )(*results)
    return mixed, gtok, ggates.T, gdown[None]


def solution(mesh):
    n, n_expert = mesh.shape["dp"], mesh.shape["expert"]
    return jax.shard_map(
        functools.partial(local, n, n_expert),
        mesh=mesh,
        in_specs=(
            P("expert", None),
            P("expert", None),
            P("expert", None),
            P("expert", None),
            P("expert", None, "dp"),
            P("expert", None, "dp"),
            P("expert", "dp", None),
        ),
        out_specs=(
            P("expert", None),
            P("expert", None),
            P("expert", None),
            P("expert", "dp", None),
        ),
        check_vma=False,
    )
```
